256 devices in a mesh: theta: 32 (over z, y_lo, core), row: 8 (over y_hi, x).
Axes of the slice: x: 4, y: 4 (y_hi: 2, y_lo: 2; y = y_hi * 2 + y_lo), z: 8, core: 2. Of those that a mesh axis runs over, the one named last changes fastest.
Arguments:
- rhs: float32 [5, 32, 256, 4096], P(None, None, 'row', 'theta'), may hold values from -8 to 8
- decay_radial: float32 [2, 5, 32], replicated, may hold values from 1 to 170
- decay_theta: float32 [2, 5, 32], replicated, may hold values from 1 to 2730
- mix_mid: float32 [5, 5, 32, 256], P(None, None, None, 'row'), may hold values from -2 to 3
- mix_out: float32 [5, 5, 32, 256], P(None, None, None, 'row'), may hold values from -2 to 3
Outputs:
- update: float32 [5, 32, 256, 4096], P(None, None, 'row', 'theta')
The draws below stay inside these ranges and needn't reach their ends.
All inputs are finite; a program needn't handle non-finite values.
Results may differ from the reference program's by a relative error of at most 0.0003.
Values sent between devices are 32-bit elements; how exact they have to be, the bound alone decides.
A program may use at most 192 MiB of HBM per device.

```python
import math
import jax
import jax.numpy as jnp
from jax import lax

VARS = 5
K = 32
NR = 256
NT = 4096


def decay_values(key, array_shape, top_value, exponent):
    spread_key = jax.random.fold_in(key, 5)
    position = jax.random.uniform(spread_key, array_shape, jnp.float32, 0.0, 1.0)
    return jnp.exp(math.log(top_value) * position ** exponent)


def draw_rhs(key, part):
    key = jax.random.fold_in(key, 11)
    rough_key, level_key = jax.random.split(key, 2)
    rough = jnp.clip(jax.random.normal(rough_key, (VARS, K, NR, NT), jnp.float32), -4.0, 4.0)
    level = jnp.clip(jax.random.normal(level_key, (VARS, K, NR, 1), jnp.float32), -2.0, 2.0)
    return rough + level


def draw_decay_radial(key, part):
    key = jax.random.fold_in(key, 23)
    top_value = float(max(3, 2 * NR // 3))
    return decay_values(key, (2, VARS, K), top_value, 1.0)


def draw_decay_theta(key, part):
    key = jax.random.fold_in(key, 29)
    top_value = float(max(3, 2 * NT // 3))
    return decay_values(key, (2, VARS, K), top_value, 1.0)


def draw_mix_mid(key, part):
    key = jax.random.fold_in(key, 31)
    off_key = jax.random.fold_in(key, 1)
    identity = jnp.eye(VARS, dtype=jnp.float32)[:, :, None, None]
    spread_part = 0.35 * jnp.clip(jax.random.normal(off_key, (VARS, VARS, K, NR), jnp.float32), -3.0, 3.0)
    return identity + spread_part


def draw_mix_out(key, part):
    key = jax.random.fold_in(key, 37)
    off_key = jax.random.fold_in(key, 1)
    identity = jnp.eye(VARS, dtype=jnp.float32)[:, :, None, None]
    spread_part = 0.35 * jnp.clip(jax.random.normal(off_key, (VARS, VARS, K, NR), jnp.float32), -3.0, 3.0)
    return identity + spread_part


def setup_inputs(seed: int = 0) -> dict:
    splits = jax.random.split(jax.random.key(seed), 6)
    return {
        "rhs": draw_rhs(jax.random.fold_in(splits[5], 71), 0),
        "decay_radial": draw_decay_radial(jax.random.fold_in(splits[5], 71), 0),
        "decay_theta": draw_decay_theta(jax.random.fold_in(splits[5], 71), 0),
        "mix_mid": draw_mix_mid(jax.random.fold_in(splits[5], 71), 0),
        "mix_out": draw_mix_out(jax.random.fold_in(splits[5], 71), 0),
    }


PRECISE = lax.Precision.HIGHEST


def radial_solve(values, decay):
    log_rates = -decay / NR
    first_rate = jnp.exp(log_rates[0])[:, :, None]
    second_rate = jnp.exp(log_rates[1])[:, :, None]
    factor = (jnp.expm1(log_rates[0]) * jnp.expm1(log_rates[1]))[:, :, None]
    radial_lines = jnp.moveaxis(values, 2, 0)
    zero_state = jnp.zeros(radial_lines.shape[1:], jnp.float32)

    def forward(state_pair, column):
        first_state = first_rate * state_pair[0] + column
        second_state = second_rate * state_pair[1] + first_state
        return (first_state, second_state), second_state

    def backward(state_pair, column):
        first_state = second_rate * state_pair[0] + column
        second_state = first_rate * state_pair[1] + first_state
        return (first_state, second_state), second_state

    forward_part = lax.scan(forward, (zero_state, zero_state), radial_lines)[1] * factor
    solved = lax.scan(backward, (zero_state, zero_state), forward_part, reverse=True)[1] * factor
    return jnp.moveaxis(solved, 0, 2)


def theta_solve(values, decay):
    log_rates = -decay / NT
    half_angles = jnp.arange(NT // 2 + 1, dtype=jnp.float32) * (math.pi / NT)
    sine_squares = jnp.sin(half_angles) ** 2
    first_rate = jnp.exp(log_rates[0])[:, :, None]
    second_rate = jnp.exp(log_rates[1])[:, :, None]
    first_gap = jnp.expm1(log_rates[0])[:, :, None]
    second_gap = jnp.expm1(log_rates[1])[:, :, None]
    symbol = (first_gap ** 2 + 4.0 * first_rate * sine_squares) * (second_gap ** 2 + 4.0 * second_rate * sine_squares)
    filter_gain = (first_gap * second_gap) ** 2 / symbol

    def plane(inputs):
        plane_values, plane_gain = inputs
        spectrum = jnp.fft.rfft(plane_values, axis=-1) * plane_gain[:, None, :]
        return jnp.fft.irfft(spectrum, n=NT, axis=-1)

    result = lax.map(plane, (jnp.moveaxis(values, 1, 0), jnp.moveaxis(filter_gain, 1, 0)))
    return jnp.moveaxis(result, 0, 1)


def reference(rhs, decay_radial, decay_theta, mix_mid, mix_out):
    radial_field = radial_solve(rhs, decay_radial)
    mixed_field = jnp.einsum("mnkr,nkrt->mkrt", mix_mid, radial_field, precision=PRECISE)
    azimuthal = theta_solve(mixed_field, decay_theta)
    return jnp.einsum("mnkr,nkrt->mkrt", mix_out, azimuthal, precision=PRECISE)
```

```python
import functools

import jax
import jax.numpy as jnp
from jax import lax
from jax.experimental import pallas as pl
from jax.experimental.pallas import tpu as pltpu
from jax.sharding import PartitionSpec as P

MESH = pl.DeviceIdType.MESH
KC = 8
SLOT = 24
F32 = jnp.float32
BF16 = jnp.bfloat16


def gap(u):
    h = 0.5 * u
    q = h * h
    series = 1.0 + q / 6.0 * (1.0 + q / 20.0 * (1.0 + q / 42.0 * (1.0 + q / 72.0)))
    return 2.0 * jnp.exp(-h) * h * series


def split(x):
    hi = x.astype(BF16)
    return hi, (x - hi.astype(F32)).astype(BF16)


def block_transfer(u1, u2, doublings):
    a, b = jnp.exp(-u1), jnp.exp(-u2)
    c = a
    q11, q12, q21, q22 = a, b, a, b
    for _ in range(doublings):
        x11, x12 = q11 * a + q12 * c, q12 * b
        x21, x22 = q21 * a + q22 * c, q22 * b
        q11, q12, q21, q22 = (
            q11 + a * x11,
            q12 + a * x12,
            q21 + c * x11 + b * x21,
            q22 + c * x12 + b * x22,
        )
        c = c * (a + b)
        a, b = a * a, b * b
    return a, b, c, q11, q12, q21, q22


def pick_lane(values, index):
    lane = lax.broadcasted_iota(jnp.int32, values.shape, 1)
    return jnp.sum(jnp.where(lane == index, values, 0.0), axis=1, keepdims=True)


def power_tables(u1, u2, n, bits):
    nf = n.astype(F32)
    a, b = jnp.exp(-nf * u1), jnp.exp(-nf * u2)
    ab, bb = jnp.exp(-u1), jnp.exp(-u2)
    pb = jnp.ones_like(ab)
    p = jnp.zeros_like(nf * u1)
    low = jnp.ones_like(p)
    for bit in range(bits):
        has = (n >> bit) & 1 == 1
        p = jnp.where(has, ab * p + low * pb, p)
        low = jnp.where(has, low * bb, low)
        pb = pb * (ab + bb)
        ab, bb = ab * ab, bb * bb
    return a, b, p


def solve_kernel(
    sizes, rhs, dr, dt, mixm, mixo, l2_out, infl_out, etab,
    xin, xm, zbuf, l2buf, ybuf, rcoef, mcoef, gtab, wtab, xhi, xlo,
    e1, rcv1, o1, rcv2, tx1, trc1, tx2, trc2,
    in_sem, s1s, s1r, s2s, s2r, t1s, t1r, t2s, t2r, out_sem, fin_sem,
):
    V, K, RL, TL, nrow, nth = sizes
    nchunk = K // KC
    me_r = lax.axis_index("row")
    me_t = lax.axis_index("theta")
    kr = KC * RL

    def in_copy(c):
        return pltpu.make_async_copy(rhs.at[:, pl.ds(c * kr, kr), :], xin.at[c], in_sem.at[c])

    for c in range(nchunk):
        in_copy(c).start()

    barrier = pltpu.get_barrier_semaphore()

    @pl.loop(1, nrow)
    def _(d):
        pl.semaphore_signal(barrier, inc=1, device_id={"row": lax.rem(me_r + d, nrow)}, device_id_type=MESH)

    @pl.loop(1, nth)
    def _(d):
        pl.semaphore_signal(barrier, inc=1, device_id={"theta": lax.rem(me_t + d, nth)}, device_id_type=MESH)

    cells_r = RL * nrow
    ur1, ur2 = dr[0] / cells_r, dr[1] / cells_r
    fr = gap(ur1) * gap(ur2)
    diag = lax.broadcasted_iota(jnp.int32, (K, K), 0) == lax.broadcasted_iota(jnp.int32, (K, K), 1)
    for j, table in enumerate((jnp.exp(-ur1), jnp.exp(-ur2), fr * fr)):
        for m in range(V):
            column = jnp.sum(
                jnp.where(diag, jnp.broadcast_to(table[m : m + 1, :], (K, K)), 0.0), axis=1, keepdims=True
            )
            rcoef[j, m] = jnp.broadcast_to(column, (K, TL))
    radial_block = block_transfer(ur1, ur2, RL.bit_length() - 1)

    def radial_pass(c, states, emit):
        r1 = [rcoef[0, m, pl.ds(c * KC, KC), :] for m in range(V)]
        r2 = [rcoef[1, m, pl.ds(c * KC, KC), :] for m in range(V)]

        def ahead(r, carry):
            out = []
            for m in range(V):
                s1, s2 = carry[m]
                s1 = r1[m] * s1 + xin[c, m, pl.ds(r, KC, stride=RL), :]
                s2 = r2[m] * s2 + s1
                ybuf[m, pl.ds(pl.multiple_of(r * KC, KC), KC), :] = s2
                out.append((s1, s2))
            return tuple(out)

        def behind(i, carry):
            r = RL - 1 - i
            out = []
            for m in range(V):
                u1, u2 = carry[m]
                u1 = r1[m] * u1 + ybuf[m, pl.ds(pl.multiple_of(r * KC, KC), KC), :]
                u2 = r2[m] * u2 + u1
                out.append((u1, u2))
            if emit is not None:
                emit(r, [pair[1] for pair in out])
            return tuple(out)

        first = lax.fori_loop(0, RL, ahead, tuple((s[0], s[1]) for s in states), unroll=4)
        second = lax.fori_loop(0, RL, behind, tuple((s[2], s[3]) for s in states), unroll=4)
        return first, second

    @pl.loop(0, nchunk)
    def _(c):
        in_copy(c).wait()
        zero = jnp.zeros((KC, TL), F32)
        first, second = radial_pass(c, [(zero,) * 4] * V, None)
        for m in range(V):
            for s, value in enumerate((first[m][0], first[m][1], second[m][0], second[m][1])):
                e1[c, pl.ds(s * V + m, KC, stride=SLOT), :] = value

        @pl.when(c == 0)
        def _():
            pl.semaphore_wait(barrier, nrow - 1 + nth - 1)

        @pl.loop(1, nrow)
        def _(d):
            p = lax.rem(me_r + d, nrow)
            pltpu.make_async_remote_copy(
                src_ref=e1.at[c, pl.ds(pl.multiple_of(p * SLOT, 8), SLOT), :],
                dst_ref=rcv1.at[c, me_r],
                send_sem=s1s.at[c],
                recv_sem=s1r.at[c],
                device_id={"row": p},
                device_id_type=MESH,
            ).start()

        pltpu.make_async_copy(
            e1.at[c, pl.ds(pl.multiple_of(me_r * SLOT, 8), SLOT), :], rcv1.at[c, me_r], s1r.at[c]
        ).start()

    cells_t = TL * nth
    ut1, ut2 = dt[0] / cells_t, dt[1] / cells_t
    lane = lax.broadcasted_iota(jnp.int32, (V, TL), 1)
    sub8 = lax.broadcasted_iota(jnp.int32, (8, TL), 0)
    lane8 = lax.broadcasted_iota(jnp.int32, (8, TL), 1)
    bits = TL.bit_length() - 1

    etab[...] = jnp.zeros_like(etab)
    wtab[...] = jnp.zeros_like(wtab)

    @pl.loop(0, K)
    def _(k):
        u1 = pick_lane(ut1, k)
        u2 = pick_lane(ut2, k)
        r1, r2 = jnp.exp(-u1), jnp.exp(-u2)
        f = gap(u1) * gap(u2)
        g12, g11, g22 = gap(u1 + u2), gap(2.0 * u1), gap(2.0 * u2)
        scale_1 = f * f * r1 / g12
        coef_a = scale_1 * (r1 / (g11 * g12) + r2 / (g12 * g22))
        coef_p = scale_1 / g22
        coef_b = f * f / (g12 * g22)
        af, bf, pf = power_tables(u1, u2, lane, bits)
        ar, br, pr = power_tables(u1, u2, TL - 1 - lane, bits)
        pf1, pr1 = r1 * pf + bf, r1 * pr + br
        h0 = coef_a * af + coef_p * pf + coef_b * bf
        e_s1 = coef_a * (r1 * af) + coef_p * pf1
        e_s2 = coef_b * (r2 * bf)
        e_t1 = coef_a * (r1 * ar) + coef_p * pr1
        e_t2 = coef_b * (r2 * br)
        h1 = e_t1 + e_t2
        for s, value in enumerate((e_s1, e_s2, e_t1, e_t2)):
            etab[k, 8 * s : 8 * s + V, :] = value
        for s, value in enumerate((ar, pr1, af, pf1)):
            hi, lo = split(value)
            wtab[k, 8 * s : 8 * s + V, :] = value
        for m in range(V):
            near = pltpu.roll(jnp.broadcast_to(h0[m : m + 1, :], (8, TL)), 0, 1, stride=1, stride_axis=0)
            far = pltpu.roll(jnp.broadcast_to(h1[m : m + 1, :], (8, TL)), 0, 1, stride=1, stride_axis=0)
            for b in range(TL // 16):
                rows = []
                for half in (0, 8):
                    shift = 16 * b + half
                    if shift:
                        left, right = pltpu.roll(far, shift, 1), pltpu.roll(near, shift, 1)
                    else:
                        left, right = far, near
                    rows.append(jnp.where(lane8 < shift + sub8, left, right))
                hi, lo = split(jnp.concatenate(rows, axis=0))
                gtab[k, m, 16 * b : 16 * b + 16, 0:TL] = hi
                gtab[k, m, 16 * b : 16 * b + 16, TL : 2 * TL] = lo

    def spread(which, table):
        @pl.loop(0, V * V)
        def _(q):
            @pl.loop(0, nchunk)
            def _(c):
                block = table[q, pl.ds(pl.multiple_of(c * KC, KC), KC), :]
                for r in range(RL):
                    mcoef[which, c, r, q] = jnp.broadcast_to(block[:, r : r + 1], (KC, TL))

    spread(0, mixm)

    @pl.loop(0, nchunk)
    def _(c):
        a, b, cc, q11, q12, q21, q22 = (
            jnp.broadcast_to(pick_lane(x, c * KC + me_r), (V, TL)) for x in radial_block
        )
        pltpu.make_async_copy(rcv1.at[c], rcv1.at[c], s1r.at[c]).wait()

        def got(d, s):
            return rcv1[c, d, s * V : s * V + V, :]

        zero = jnp.zeros((V, TL), F32)
        sa, sb = [zero], [zero]
        for d in range(nrow - 1):
            sa.append(a * sa[d] + got(d, 0))
            sb.append(b * sb[d] + cc * sa[d] + got(d, 1))
        ta, tb = zero, zero
        for d in range(nrow - 1, -1, -1):
            for s, value in enumerate((sa[d], sb[d], ta, tb)):
                o1[c, d, s * V : s * V + V, :] = value
            if d:
                ta, tb = (
                    a * ta + got(d, 2) + q11 * sa[d] + q12 * sb[d],
                    b * tb + cc * ta + got(d, 3) + q21 * sa[d] + q22 * sb[d],
                )

        @pl.loop(1, nrow)
        def _(i):
            p = lax.rem(me_r + i, nrow)
            pltpu.make_async_remote_copy(
                src_ref=o1.at[c, p],
                dst_ref=rcv2.at[c, pl.ds(pl.multiple_of(me_r * SLOT, 8), SLOT), :],
                send_sem=s2s.at[c],
                recv_sem=s2r.at[c],
                device_id={"row": p},
                device_id_type=MESH,
            ).start()

        pltpu.make_async_copy(
            o1.at[c, me_r], rcv2.at[c, pl.ds(pl.multiple_of(me_r * SLOT, 8), SLOT), :], s2r.at[c]
        ).start()

    spread(1, mixo)

    @pl.loop(0, nchunk)
    def _(c):
        pltpu.make_async_copy(rcv2.at[c], rcv2.at[c], s2r.at[c]).wait()
        states = [
            tuple(rcv2[c, pl.ds(s * V + m, KC, stride=SLOT), :] for s in range(4)) for m in range(V)
        ]
        f2 = [rcoef[2, m, pl.ds(c * KC, KC), :] for m in range(V)]

        def emit(r, z):
            z = [f2[m] * z[m] for m in range(V)]
            for m in range(V):
                total = mcoef[0, c, r, m * V] * z[0]
                for n in range(1, V):
                    total = total + mcoef[0, c, r, m * V + n] * z[n]
                xm[m, pl.ds(r, KC, stride=RL), :] = total

        radial_pass(c, states, emit)

        @pl.loop(0, KC)
        def _(kk):
            k = c * KC + kk
            rows = pl.ds(pl.multiple_of(kk * RL, RL), RL)
            hi, lo = split(jnp.concatenate([xm[m, rows, :] for m in range(V)], axis=0))
            xhi[k] = hi
            xlo[k] = lo
            whi, wlo = split(wtab[k])
            dims = (((1,), (1,)), ((), ()))
            out = lax.dot_general(jnp.concatenate([whi, wlo], axis=0), hi, dims, preferred_element_type=F32)
            out = out[0:32] + out[32:64] + lax.dot_general(whi, lo, dims, preferred_element_type=F32)
            both = []
            for s in range(4):
                first = out[8 * s : 8 * s + 8, 0:TL]
                last = jnp.concatenate([out[8 * s : 8 * s + 8, TL : TL + RL]] * 4, axis=1)
                both.append(jnp.where(sub8 == V - 1, last, first))
            message = jnp.zeros((8, TL), F32)
            for j in range(4):
                picked = both[(j + 3) % 4]
                for q in range(3):
                    picked = jnp.where(sub8 % 4 == q, both[(j + q) % 4], picked)
                moved = pltpu.roll(picked, j * RL, 1) if j else picked
                message = jnp.where(lane8 // RL == (sub8 + j) % 4, moved, message)
            tx1[k] = message[0:V]

            @pl.when(k == me_t)
            def _():
                pltpu.make_async_copy(tx1.at[k], trc1.at[me_t], t1r).start()

            @pl.when(k != me_t)
            def _():
                pltpu.make_async_remote_copy(
                    src_ref=tx1.at[k],
                    dst_ref=trc1.at[me_t],
                    send_sem=t1s,
                    recv_sem=t1r,
                    device_id={"theta": k},
                    device_id_type=MESH,
                ).start()

    def out_copy(c):
        return pltpu.make_async_copy(l2buf.at[c], l2_out.at[:, pl.ds(c * kr, kr), :], out_sem.at[c])

    def local_solve(c):
        @pl.loop(0, KC)
        def _(kk):
            k = c * KC + kk
            for m in range(V):
                hi = xhi[k, m * RL : m * RL + RL, :]
                lo = xlo[k, m * RL : m * RL + RL, :]
                ghi = gtab[k, m, :, 0:TL]
                glo = gtab[k, m, :, TL : 2 * TL]
                z = jnp.dot(jnp.concatenate([hi, lo], axis=0), ghi, preferred_element_type=F32)
                z = z[0:RL] + z[RL : 2 * RL] + jnp.dot(hi, glo, preferred_element_type=F32)
                zbuf[m, pl.ds(pl.multiple_of(kk * RL, RL), RL), :] = z

        def mix(r, carry):
            z = [zbuf[n, pl.ds(r, KC, stride=RL), :] for n in range(V)]
            for m in range(V):
                total = mcoef[1, c, r, m * V] * z[0]
                for n in range(1, V):
                    total = total + mcoef[1, c, r, m * V + n] * z[n]
                l2buf[c, m, pl.ds(r, KC, stride=RL), :] = total
            return carry

        lax.fori_loop(0, RL, mix, 0, unroll=4)
        out_copy(c).start()

    local_solve(0)

    u1, u2 = pick_lane(ut1, me_t), pick_lane(ut2, me_t)
    a, b, cc = (jnp.broadcast_to(x, (V, TL)) for x in block_transfer(u1, u2, bits)[:3])
    u1, u2 = jnp.broadcast_to(u1, (V, TL)), jnp.broadcast_to(u2, (V, TL))
    around_1 = 1.0 / (1.0 - jnp.exp(-cells_t * u1))
    around_2 = 1.0 / (1.0 - jnp.exp(-cells_t * u2))
    pltpu.make_async_copy(trc1, trc1, t1r).wait()
    forward = lane < 2 * RL
    entering = [jnp.where(forward, trc1[i], trc1[nth - 1 - i]) for i in range(nth)]

    def cycle(rate, decay, around, terms):
        chain = [jnp.zeros((V, TL), F32)]
        for i in range(nth):
            chain.append(rate * chain[i] + terms[i])
        start = chain[nth] * around
        return [chain[i] + jnp.exp(-(TL * i) * decay) * start for i in range(nth)]

    one = cycle(a, u1, around_1, entering)
    two = cycle(b, u2, around_2, [entering[i] + cc * pltpu.roll(one[i], RL, 1) for i in range(nth)])
    even = (lane // RL) % 2 == 0
    state = [jnp.where(even, one[i], two[i]) for i in range(nth)]
    for d in range(nth):
        tx2[d] = jnp.where(forward, state[d], state[nth - 1 - d])

    @pl.loop(1, nth)
    def _(i):
        d = lax.rem(me_t + i, nth)
        pltpu.make_async_remote_copy(
            src_ref=tx2.at[d],
            dst_ref=trc2.at[me_t],
            send_sem=t2s,
            recv_sem=t2r,
            device_id={"theta": d},
            device_id_type=MESH,
        ).start()

    pltpu.make_async_copy(tx2.at[me_t], trc2.at[me_t], t2r).start()

    @pl.loop(1, nchunk)
    def _(c):
        local_solve(c)

    pltpu.make_async_copy(trc2, trc2, t2r).wait()
    final = pltpu.make_async_copy(trc2, infl_out, fin_sem)
    final.start()

    @pl.loop(0, nchunk)
    def _(c):
        sent = rcv1.at[c, pl.ds(0, nrow - 1)]
        pltpu.make_async_copy(sent, sent, s1s.at[c]).wait()
        pltpu.make_async_copy(sent, sent, s2s.at[c]).wait()
        out_copy(c).wait()

    sent = trc1.at[pl.ds(0, nth - 1)]
    pltpu.make_async_copy(sent, sent, t1s).wait()
    pltpu.make_async_copy(sent, sent, t2s).wait()
    final.wait()


def finish_kernel(sizes, l2, infl, etab, mixo, out):
    V, K, RL, TL, nrow, nth = sizes
    kb = infl.shape[0]
    dims = (((0,), (0,)), ((), ()))
    for k in range(kb):
        inflow = infl[k]
        states = [inflow[:, s * RL : s * RL + RL] for s in range(4)]
        pad = jnp.zeros((8 - V, RL), F32)
        ehi, elo = split(etab[k])
        weights = jnp.concatenate([ehi, ehi, elo], axis=0)
        for m in range(V):
            gain = jnp.concatenate([mixo[m * V + n, k : k + 1, :] for n in range(V)], axis=0)
            parts = []
            for s in range(4):
                parts += [states[s] * gain, pad]
            hi, lo = split(jnp.concatenate(parts, axis=0))
            left = jnp.concatenate([hi, lo, hi], axis=0)
            rows = slice(k * RL, k * RL + RL)
            out[m, rows, :] = l2[m, rows, :] + lax.dot_general(left, weights, dims, preferred_element_type=F32)


def body(nrow, nth, rhs, dr, dt, mixm, mixo):
    V, K, RL, TL = rhs.shape
    sizes = (V, K, RL, TL, nrow, nth)
    nchunk = K // KC
    kr = KC * RL
    field = jax.ShapeDtypeStruct((V, K * RL, TL), F32)
    vmem = pl.BlockSpec(memory_space=pltpu.VMEM)
    hbm = pl.BlockSpec(memory_space=pl.ANY)
    mixm = mixm.reshape(V * V, K, RL)
    mixo = mixo.reshape(V * V, K, RL)
    dma = pltpu.SemaphoreType.DMA
    l2, infl, etab = pl.pallas_call(
        functools.partial(solve_kernel, sizes),
        out_shape=(
            field,
            jax.ShapeDtypeStruct((K, V, TL), F32),
            jax.ShapeDtypeStruct((K, 32, TL), F32),
        ),
        in_specs=[hbm, vmem, vmem, vmem, vmem],
        out_specs=(hbm, hbm, vmem),
        scratch_shapes=[
            pltpu.VMEM((nchunk, V, kr, TL), F32),
            pltpu.VMEM((V, kr, TL), F32),
            pltpu.VMEM((V, kr, TL), F32),
            pltpu.VMEM((nchunk, V, kr, TL), F32),
            pltpu.VMEM((V, kr, TL), F32),
            pltpu.VMEM((3, V, K, TL), F32),
            pltpu.VMEM((2, nchunk, RL, V * V, KC, TL), F32),
            pltpu.VMEM((K, V, TL, 2 * TL), BF16),
            pltpu.VMEM((K, 32, TL), F32),
            pltpu.VMEM((K, V * RL, TL), BF16),
            pltpu.VMEM((K, V * RL, TL), BF16),
            pltpu.VMEM((nchunk, nrow * SLOT, TL), F32),
            pltpu.VMEM((nchunk, nrow, SLOT, TL), F32),
            pltpu.VMEM((nchunk, nrow, SLOT, TL), F32),
            pltpu.VMEM((nchunk, nrow * SLOT, TL), F32),
            pltpu.VMEM((K, V, TL), F32),
            pltpu.VMEM((nth, V, TL), F32),
            pltpu.VMEM((nth, V, TL), F32),
            pltpu.VMEM((K, V, TL), F32),
            dma((nchunk,)), dma((nchunk,)), dma((nchunk,)), dma((nchunk,)), dma((nchunk,)),
            dma, dma, dma, dma, dma((nchunk,)), dma,
        ],
        compiler_params=pltpu.CompilerParams(
            collective_id=0, has_side_effects=True, vmem_limit_bytes=60 * 1024 * 1024
        ),
        name="solve",
    )(rhs.reshape(V, K * RL, TL), dr, dt, mixm, mixo)
    kb = KC
    out = pl.pallas_call(
        functools.partial(finish_kernel, sizes),
        grid=(K // kb,),
        out_shape=field,
        in_specs=[
            pl.BlockSpec((V, kb * RL, TL), lambda i: (0, i, 0)),
            pl.BlockSpec((kb, V, TL), lambda i: (i, 0, 0)),
            pl.BlockSpec((kb, 32, TL), lambda i: (i, 0, 0)),
            pl.BlockSpec((V * V, kb, RL), lambda i: (0, i, 0)),
        ],
        out_specs=pl.BlockSpec((V, kb * RL, TL), lambda i: (0, i, 0)),
        compiler_params=pltpu.CompilerParams(vmem_limit_bytes=32 * 1024 * 1024),
        name="finish",
    )(l2, infl, etab, mixo)
    return out.reshape(V, K, RL, TL)


def solution(mesh):
    return jax.shard_map(
        functools.partial(body, mesh.shape["row"], mesh.shape["theta"]),
        mesh=mesh,
        in_specs=(
            P(None, None, "row", "theta"),
            P(),
            P(),
            P(None, None, None, "row"),
            P(None, None, None, "row"),
        ),
        out_specs=P(None, None, "row", "theta"),
        check_vma=False,
    )
```

```python
import functools

import jax
import jax.numpy as jnp
from jax import lax
from jax.experimental import pallas as pl
from jax.experimental.pallas import tpu as pltpu
from jax.sharding import PartitionSpec as P

MESH = pl.DeviceIdType.MESH
KC = 8
SLOT = 24
STATES = 4
LINE = 32
F32 = jnp.float32
BF16 = jnp.bfloat16


def gap(u):
    h = 0.5 * u
    q = h * h
    series = 1.0 + q / 6.0 * (1.0 + q / 20.0 * (1.0 + q / 42.0 * (1.0 + q / 72.0)))
    return 2.0 * jnp.exp(-h) * h * series


def split(x):
    hi = x.astype(BF16)
    return hi, (x - hi.astype(F32)).astype(BF16)


def block_transfer(u1, u2, doublings):
    a, b = jnp.exp(-u1), jnp.exp(-u2)
    c = a
    q11, q12, q21, q22 = a, b, a, b
    for _ in range(doublings):
        x11, x12 = q11 * a + q12 * c, q12 * b
        x21, x22 = q21 * a + q22 * c, q22 * b
        q11, q12, q21, q22 = (
            q11 + a * x11,
            q12 + a * x12,
            q21 + c * x11 + b * x21,
            q22 + c * x12 + b * x22,
        )
        c = c * (a + b)
        a, b = a * a, b * b
    return a, b, c, q11, q12, q21, q22


def pick_lane(values, index):
    lane = lax.broadcasted_iota(jnp.int32, values.shape, 1)
    return jnp.sum(jnp.where(lane == index, values, 0.0), axis=1, keepdims=True)


def power_tables(u1, u2, n, bits):
    nf = n.astype(F32)
    a, b = jnp.exp(-nf * u1), jnp.exp(-nf * u2)
    ab, bb = jnp.exp(-u1), jnp.exp(-u2)
    pb = jnp.ones_like(ab)
    p = jnp.zeros_like(nf * u1)
    low = jnp.ones_like(p)
    for bit in range(bits):
        has = (n >> bit) & 1 == 1
        p = jnp.where(has, ab * p + low * pb, p)
        low = jnp.where(has, low * bb, low)
        pb = pb * (ab + bb)
        ab, bb = ab * ab, bb * bb
    return a, b, p


def solve_kernel(
    sizes, rhs, decay_r, decay_t, mixm, mixo, l2, infl, etab, gain,
    xin, xbuf, zbuf, ybuf, rcoef, ucol, h0tab, h1tab, wtab, wturn, gtab, mcat, mrows, xsplit,
    e1, rcv1, o1, rcv2, tx1, trc1, tx2, trc2,
    in_sem, s1s, s1r, s2s, s2r, t1s, t1r, t2s, t2r, fin_sem,
):
    V, K, RL, TL, nrow, nth = sizes
    nchunk = K // KC
    me_r = lax.axis_index("row")
    me_t = lax.axis_index("theta")
    kr = KC * RL
    dr = [decay_r[:, j, :] for j in range(2)]
    dt = [decay_t[:, j, :] for j in range(2)]

    def in_copy(c):
        return pltpu.make_async_copy(rhs.at[:, pl.ds(c * kr, kr), :], xin.at[c], in_sem.at[c])

    for c in range(nchunk):
        in_copy(c).start()

    barrier = pltpu.get_barrier_semaphore()

    @pl.loop(1, nrow)
    def _(d):
        pl.semaphore_signal(barrier, inc=1, device_id={"row": lax.rem(me_r + d, nrow)}, device_id_type=MESH)

    @pl.loop(1, nth)
    def _(d):
        pl.semaphore_signal(barrier, inc=1, device_id={"theta": lax.rem(me_t + d, nth)}, device_id_type=MESH)

    cells_r = RL * nrow
    ur1, ur2 = dr[0] / cells_r, dr[1] / cells_r
    fr = gap(ur1) * gap(ur2)
    diag = lax.broadcasted_iota(jnp.int32, (K, K), 0) == lax.broadcasted_iota(jnp.int32, (K, K), 1)

    def to_columns(table, ref, j):
        for m in range(V):
            column = jnp.sum(
                jnp.where(diag, jnp.broadcast_to(table[m : m + 1, :], (K, K)), 0.0), axis=1, keepdims=True
            )
            ref[j, m] = jnp.broadcast_to(column, (K, TL))

    for j, table in enumerate((jnp.exp(-ur1), jnp.exp(-ur2), fr * fr)):
        to_columns(table, rcoef, j)
    radial_block = block_transfer(ur1, ur2, RL.bit_length() - 1)

    def radial_pass(c, states, emit):
        r1 = [rcoef[0, m, pl.ds(c * KC, KC), :] for m in range(V)]
        r2 = [rcoef[1, m, pl.ds(c * KC, KC), :] for m in range(V)]

        def ahead(r, carry):
            out = []
            for m in range(V):
                s1, s2 = carry[m]
                s1 = r1[m] * s1 + xin[c, m, pl.ds(r, KC, stride=RL), :]
                s2 = r2[m] * s2 + s1
                ybuf[m, pl.ds(pl.multiple_of(r * KC, KC), KC), :] = s2
                out.append((s1, s2))
            return tuple(out)

        def behind(i, carry):
            r = RL - 1 - i
            out = []
            for m in range(V):
                u1, u2 = carry[m]
                u1 = r1[m] * u1 + ybuf[m, pl.ds(pl.multiple_of(r * KC, KC), KC), :]
                u2 = r2[m] * u2 + u1
                out.append((u1, u2))
            if emit is not None:
                emit(r, [pair[1] for pair in out])
            return tuple(out)

        first = lax.fori_loop(0, RL, ahead, tuple((s[0], s[1]) for s in states), unroll=8)
        second = lax.fori_loop(0, RL, behind, tuple((s[2], s[3]) for s in states), unroll=8)
        return first, second

    @pl.loop(0, nchunk)
    def _(c):
        in_copy(c).wait()
        zero = jnp.zeros((KC, TL), F32)
        first, second = radial_pass(c, [(zero,) * 4] * V, None)
        for m in range(V):
            for s, value in enumerate((first[m][0], first[m][1], second[m][0], second[m][1])):
                e1[c, pl.ds(s * V + m, KC, stride=SLOT), :] = value

    cells_t = TL * nth
    ut1, ut2 = dt[0] / cells_t, dt[1] / cells_t
    to_columns(ut1, ucol, 0)
    to_columns(ut2, ucol, 1)
    lane32 = lax.broadcasted_iota(jnp.int32, (RL, TL), 1)
    lane8 = lax.broadcasted_iota(jnp.int32, (8, TL), 1)
    bits = TL.bit_length() - 1
    etab[...] = jnp.zeros_like(etab)
    wtab[...] = jnp.zeros_like(wtab)

    def tables(q, carry):
        m, c = q // nchunk, q % nchunk
        rows = pl.ds(pl.multiple_of(c * KC, KC), KC)
        u1, u2 = ucol[0, m, rows, :], ucol[1, m, rows, :]
        r1, r2 = jnp.exp(-u1), jnp.exp(-u2)
        f = gap(u1) * gap(u2)
        i12, i11, i22 = 1.0 / gap(u1 + u2), 1.0 / gap(2.0 * u1), 1.0 / gap(2.0 * u2)
        scale_1 = f * f * r1 * i12
        coef_a = scale_1 * i12 * (r1 * i11 + r2 * i22)
        coef_p = scale_1 * i22
        coef_b = f * f * i12 * i22
        af, bf, pf = power_tables(u1, u2, lane8, bits)
        ar, br, pr = power_tables(u1, u2, TL - 1 - lane8, bits)
        pf1, pr1 = r1 * pf + bf, r1 * pr + br
        e_t1 = coef_a * (r1 * ar) + coef_p * pr1
        e_t2 = coef_b * (r2 * br)
        h0tab[m, rows, :] = coef_a * af + coef_p * pf + coef_b * bf
        h1tab[m, rows, :] = e_t1 + e_t2
        e_s1 = coef_a * (r1 * af) + coef_p * pf1
        e_s2 = coef_b * (r2 * bf)
        for s, value in enumerate((e_s1, e_s2, e_t1, e_t2)):
            etab[pl.ds(c * KC * 32 + 8 * s + m, KC, stride=32), :] = value
        for s, value in enumerate((ar, pr1, af, pf1)):
            wtab[pl.ds(c * KC * 32 + 8 * s + m, KC, stride=32), :] = value
        return carry

    lax.fori_loop(0, V * nchunk, tables, 0, unroll=2)

    tile = TL // LINE
    for j in range(K // tile):
        hi, lo = split(wtab[j * TL : (j + 1) * TL, :].T)
        wturn[j] = jnp.concatenate([hi, hi, lo], axis=0)

    for which, table in enumerate((mixm, mixo)):
        for m in range(V):
            four = jnp.concatenate([table[m * V + n] for n in range(V - 1)], axis=1)
            last = table[m * V + V - 1]
            four_hi = four.astype(BF16).astype(F32)
            last_hi = last.astype(BF16).astype(F32)
            last = jnp.concatenate([last_hi, last_hi, last - last_hi, jnp.zeros_like(last)], axis=1)
            mcat[which, m, :, 0:TL] = four_hi
            mcat[which, m, :, TL : 2 * TL] = four - four_hi
            mcat[which, m, :, 2 * TL : 3 * TL] = last
    on_diagonal = (
        lax.broadcasted_iota(jnp.int32, (RL, 3 * TL), 0) == lax.broadcasted_iota(jnp.int32, (RL, 3 * TL), 1) % RL
    )

    def mix(which, k, field):
        hi, lo = split(field)
        four = (V - 1) * RL
        right = jnp.concatenate(
            [hi[0:four], lo[0:four], hi[0:four], hi[four:], lo[four:], hi[four:], jnp.zeros((RL, TL), BF16)], axis=0
        )
        left = []
        for m in range(V):
            row = jnp.broadcast_to(mcat[which, m, pl.ds(k, 1), :], (RL, 3 * TL))
            left.append(jnp.where(on_diagonal, row, 0.0).astype(BF16))
        left = jnp.concatenate(left, axis=0)
        left = jnp.concatenate([left[:, 0:TL], left], axis=1)
        return jnp.dot(left, right, preferred_element_type=F32)

    pl.semaphore_wait(barrier, nrow - 1 + nth - 1)

    @pl.loop(0, nchunk)
    def _(c):
        @pl.loop(1, nrow)
        def _(d):
            p = lax.rem(me_r + d, nrow)
            pltpu.make_async_remote_copy(
                src_ref=e1.at[c, pl.ds(pl.multiple_of(p * SLOT, 8), SLOT), :],
                dst_ref=rcv1.at[c, me_r],
                send_sem=s1s.at[c],
                recv_sem=s1r.at[c],
                device_id={"row": p},
                device_id_type=MESH,
            ).start()

        pltpu.make_async_copy(
            e1.at[c, pl.ds(pl.multiple_of(me_r * SLOT, 8), SLOT), :], rcv1.at[c, me_r], s1r.at[c]
        ).start()

    lane16 = lax.broadcasted_iota(jnp.int32, (16, TL), 1)
    sub16 = lax.broadcasted_iota(jnp.int32, (16, TL), 0)

    def toeplitz(k):
        for m in range(V):
            near = pltpu.roll(jnp.broadcast_to(h0tab[m, pl.ds(k, 1), :], (16, TL)), 0, 1, stride=1, stride_axis=0)
            far = pltpu.roll(jnp.broadcast_to(h1tab[m, pl.ds(k, 1), :], (16, TL)), 0, 1, stride=1, stride_axis=0)
            near = jnp.where(lane16 < sub16, far, near)
            for part, (n, f) in enumerate(zip(split(near), split(far))):
                for b in range(TL // 16):
                    rows = pltpu.roll(jnp.where(lane16 >= TL - 16 * b, f, n), 16 * b, 1) if b else n
                    gtab[k, m, 16 * b : 16 * b + 16, part * TL : part * TL + TL] = rows

    ready = K * 9 // 16

    @pl.loop(0, ready)
    def _(k):
        toeplitz(k)

    mrows[...] = jnp.zeros_like(mrows)
    for m in range(V):
        for n in range(V):
            mrows[pl.ds(m * K * 8 + n, K, stride=8), 0:RL] = mixo[m * V + n]
    group = 8 * TL // LINE
    source = lax.broadcasted_iota(jnp.int32, (TL, TL), 0)
    target = lax.broadcasted_iota(jnp.int32, (TL, TL), 1)
    source_rows = 8 * (target // LINE) + target % 8
    turned = []
    for m in range(V):
        for j in range(K * 8 // TL):
            turned.append(mrows[pl.ds(m * K * 8 + j * TL, TL), :].T[0:RL])
    hi, lo = split(jnp.concatenate(turned, axis=0))
    halves = jnp.concatenate([hi, lo], axis=1)
    for q in range(TL // group):
        pick = jnp.where(source == source_rows + q * group, 1.0, 0.0).astype(BF16)
        spread_rows = jnp.dot(halves, jnp.concatenate([pick, pick], axis=0), preferred_element_type=F32)
        for m in range(V):
            for j in range(K * 8 // TL):
                i = m * (K * 8 // TL) + j
                gain[j * (TL // group) + q, m * RL : m * RL + RL, :] = spread_rows[i * RL : i * RL + RL]

    @pl.loop(0, nchunk)
    def _(c):
        a, b, cc, q11, q12, q21, q22 = (
            jnp.broadcast_to(pick_lane(x, c * KC + me_r), (V, TL)) for x in radial_block
        )
        pltpu.make_async_copy(rcv1.at[c], rcv1.at[c], s1r.at[c]).wait()

        def got(d, s):
            return rcv1[c, d, s * V : s * V + V, :]

        zero = jnp.zeros((V, TL), F32)
        sa, sb = [zero], [zero]
        for d in range(nrow - 1):
            sa.append(a * sa[d] + got(d, 0))
            sb.append(b * sb[d] + cc * sa[d] + got(d, 1))
        ta, tb = zero, zero
        for d in range(nrow - 1, -1, -1):
            for s, value in enumerate((sa[d], sb[d], ta, tb)):
                o1[c, d, s * V : s * V + V, :] = value
            if d:
                ta, tb = (
                    a * ta + got(d, 2) + q11 * sa[d] + q12 * sb[d],
                    b * tb + cc * ta + got(d, 3) + q21 * sa[d] + q22 * sb[d],
                )

        @pl.loop(1, nrow)
        def _(i):
            p = lax.rem(me_r + i, nrow)
            pltpu.make_async_remote_copy(
                src_ref=o1.at[c, p],
                dst_ref=rcv2.at[c, pl.ds(pl.multiple_of(me_r * SLOT, 8), SLOT), :],
                send_sem=s2s.at[c],
                recv_sem=s2r.at[c],
                device_id={"row": p},
                device_id_type=MESH,
            ).start()

        pltpu.make_async_copy(
            o1.at[c, me_r], rcv2.at[c, pl.ds(pl.multiple_of(me_r * SLOT, 8), SLOT), :], s2r.at[c]
        ).start()

    @pl.loop(ready, K)
    def _(k):
        toeplitz(k)

    @pl.loop(0, nchunk)
    def _(c):
        pltpu.make_async_copy(rcv2.at[c], rcv2.at[c], s2r.at[c]).wait()
        states = [
            tuple(rcv2[c, pl.ds(s * V + m, KC, stride=SLOT), :] for s in range(4)) for m in range(V)
        ]
        f2 = [rcoef[2, m, pl.ds(c * KC, KC), :] for m in range(V)]

        def emit(r, z):
            for m in range(V):
                xbuf[m, pl.ds(pl.multiple_of(r * KC, KC), KC), :] = f2[m] * z[m]

        radial_pass(c, states, emit)

        def leaving(j, carry):
            total = jnp.zeros((RL, TL), F32)
            for kk in range(tile):
                k = c * KC + j * tile + kk
                field = [xbuf[m, pl.ds(j * tile + kk, RL, stride=KC), :] for m in range(V)]
                hi, lo = split(mix(0, k, jnp.concatenate(field, axis=0)))
                xsplit[k, :, 0:TL] = hi
                xsplit[k, :, TL : 2 * TL] = lo
                out = jnp.dot(
                    jnp.concatenate([hi, lo, hi], axis=1), wturn[c * (KC // tile) + j], preferred_element_type=F32
                )
                for m in range(V):
                    mine = (lane32 // LINE == kk) & (lane32 % 8 == m)
                    total = total + jnp.where(mine, out[m * RL : m * RL + RL], 0.0)
            tx1[pl.ds(c * (KC // tile) + j, RL, stride=8), :] = total
            return carry

        lax.fori_loop(0, KC // tile, leaving, 0, unroll=True)

    @pl.loop(1, nth)
    def _(i):
        p = lax.rem(me_t + i, nth)
        pltpu.make_async_remote_copy(
            src_ref=tx1.at[pl.ds(pl.multiple_of(p * 8, 8), 8), :],
            dst_ref=trc1.at[me_t],
            send_sem=t1s,
            recv_sem=t1r,
            device_id={"theta": p},
            device_id_type=MESH,
        ).start()

    pltpu.make_async_copy(tx1.at[pl.ds(pl.multiple_of(me_t * 8, 8), 8), :], trc1.at[me_t], t1r).start()

    def local_solve(c):
        def solve(kk, carry):
            k = c * KC + kk
            for m in range(V):
                hi = xsplit[k, m * RL : m * RL + RL, 0:TL]
                lo = xsplit[k, m * RL : m * RL + RL, TL : 2 * TL]
                z = jnp.dot(jnp.concatenate([hi, lo], axis=0), gtab[k, m], preferred_element_type=F32)
                z = z[0:RL, 0:TL] + z[RL : 2 * RL, 0:TL] + z[0:RL, TL : 2 * TL]
                zbuf[m, pl.ds(pl.multiple_of(kk * RL, RL), RL), :] = z
            return carry

        lax.fori_loop(0, KC, solve, 0, unroll=4)

        def out_mix(kk, carry):
            rows = pl.ds(pl.multiple_of(kk * RL, RL), RL)
            field = mix(1, c * KC + kk, jnp.concatenate([zbuf[n, rows, :] for n in range(V)], axis=0))
            for m in range(V):
                l2[m, pl.ds(pl.multiple_of((c * KC + kk) * RL, RL), RL), :] = field[m * RL : m * RL + RL]
            return carry

        lax.fori_loop(0, KC, out_mix, 0, unroll=4)

    local_solve(0)

    u1, u2 = jnp.ones((8, TL), F32), jnp.ones((8, TL), F32)
    for kk in range(tile):
        for m in range(V):
            mine = (lane8 // LINE == kk) & (lane8 % 8 == m)
            u1 = jnp.where(mine, ucol[0, m, pl.ds(kk, 8, stride=tile), :], u1)
            u2 = jnp.where(mine, ucol[1, m, pl.ds(kk, 8, stride=tile), :], u2)
    a, b, cc = block_transfer(u1, u2, bits)[:3]
    around_1 = 1.0 / (1.0 - jnp.exp(-cells_t * u1))
    around_2 = 1.0 / (1.0 - jnp.exp(-cells_t * u2))
    pltpu.make_async_copy(trc1, trc1, t1r).wait()
    forward = lane8 % LINE < LINE // 2
    entering = [jnp.where(forward, trc1[i], trc1[nth - 1 - i]) for i in range(nth)]

    def cycle(rate, decay, around, terms):
        chain = [jnp.zeros((8, TL), F32)]
        for i in range(nth):
            chain.append(rate * chain[i] + terms[i])
        start = chain[nth] * around
        return [chain[i] + jnp.exp(-(TL * i) * decay) * start for i in range(nth)]

    one = cycle(a, u1, around_1, entering)
    two = cycle(b, u2, around_2, [entering[i] + cc * pltpu.roll(one[i], 8, 1) for i in range(nth)])
    even = lane8 // 8 % 2 == 0
    state = [jnp.where(even, one[i], two[i]) for i in range(nth)]
    for d in range(nth):
        tx2[d] = jnp.where(forward, state[d], state[nth - 1 - d])

    @pl.loop(1, nth)
    def _(i):
        d = lax.rem(me_t + i, nth)
        pltpu.make_async_remote_copy(
            src_ref=tx2.at[d],
            dst_ref=trc2.at[pl.ds(pl.multiple_of(me_t * 8, 8), 8), :],
            send_sem=t2s,
            recv_sem=t2r,
            device_id={"theta": d},
            device_id_type=MESH,
        ).start()

    pltpu.make_async_copy(tx2.at[me_t], trc2.at[pl.ds(pl.multiple_of(me_t * 8, 8), 8), :], t2r).start()

    @pl.loop(1, nchunk)
    def _(c):
        local_solve(c)

    pltpu.make_async_copy(trc2, trc2, t2r).wait()
    final = pltpu.make_async_copy(trc2, infl, fin_sem)
    final.start()

    @pl.loop(0, nchunk)
    def _(c):
        sent = rcv1.at[c, pl.ds(0, nrow - 1)]
        pltpu.make_async_copy(sent, sent, s1s.at[c]).wait()
        pltpu.make_async_copy(sent, sent, s2s.at[c]).wait()

    sent = trc1.at[pl.ds(0, nth - 1)]
    pltpu.make_async_copy(sent, sent, t1s).wait()
    pltpu.make_async_copy(sent, sent, t2s).wait()
    final.wait()


def finish_kernel(sizes, l2, infl, etab, gain, out, buf, sem):
    V, K, RL, TL, nrow, nth = sizes
    tile = TL // LINE
    kr = tile * RL
    row = lax.broadcasted_iota(jnp.int32, (TL, TL), 0) // LINE

    def out_copy(j):
        rows = pl.ds(pl.multiple_of(j * kr, kr), kr)
        return pltpu.make_async_copy(buf.at[:, rows, :], out.at[:, rows, :], sem.at[j])

    @pl.loop(0, K // tile)
    def _(j):
        state = infl[pl.ds(j, RL, stride=8), :]
        hi, lo = split(gain[j] * jnp.concatenate([state] * V, axis=0))
        left = jnp.concatenate([hi, lo, hi], axis=1)
        response = etab[pl.ds(pl.multiple_of(j * TL, TL), TL), :]
        for kk in range(tile):
            ehi, elo = split(jnp.where(row == kk, response, 0.0))
            inflow = jnp.dot(left, jnp.concatenate([ehi, ehi, elo], axis=0), preferred_element_type=F32)
            rows = pl.ds(pl.multiple_of(j * kr + kk * RL, RL), RL)
            for m in range(V):
                buf[m, rows, :] = l2[m, rows, :] + inflow[m * RL : m * RL + RL]
        out_copy(j).start()

    @pl.loop(0, K // tile)
    def _(j):
        out_copy(j).wait()


def body(nrow, nth, rhs, dr, dt, mixm, mixo):
    V, K, RL, TL = rhs.shape
    sizes = (V, K, RL, TL, nrow, nth)
    nchunk = K // KC
    kr = KC * RL
    field = jax.ShapeDtypeStruct((V, K * RL, TL), F32)
    vmem = pl.BlockSpec(memory_space=pltpu.VMEM)
    hbm = pl.BlockSpec(memory_space=pl.ANY)
    mixm = mixm.reshape(V * V, K, RL)
    mixo = mixo.reshape(V * V, K, RL)
    dma = pltpu.SemaphoreType.DMA
    nline = K * LINE // TL
    l2, infl, etab, gain = pl.pallas_call(
        functools.partial(solve_kernel, sizes),
        out_shape=(
            pltpu.VMEM((V, K * RL, TL), F32),
            pltpu.VMEM((nth * 8, TL), F32),
            pltpu.VMEM((K * LINE, TL), F32),
            pltpu.VMEM((nline, V * RL, TL), F32),
        ),
        in_specs=[pl.BlockSpec(memory_space=pltpu.HBM), vmem, vmem, vmem, vmem],
        out_specs=(vmem, vmem, vmem, vmem),
        scratch_shapes=[
            pltpu.VMEM((nchunk, V, kr, TL), F32),
            pltpu.VMEM((V, kr, TL), F32),
            pltpu.VMEM((V, kr, TL), F32),
            pltpu.VMEM((V, kr, TL), F32),
            pltpu.VMEM((3, V, K, TL), F32),
            pltpu.VMEM((2, V, K, TL), F32),
            pltpu.VMEM((V, K, TL), F32),
            pltpu.VMEM((V, K, TL), F32),
            pltpu.VMEM((K * LINE, TL), F32),
            pltpu.VMEM((nline, 3 * TL, TL), BF16),
            pltpu.VMEM((K, V, TL, 2 * TL), BF16),
            pltpu.VMEM((2, V, K, 3 * TL), F32),
            pltpu.VMEM((V * K * 8, TL), F32),
            pltpu.VMEM((K, V * RL, 2 * TL), BF16),
            pltpu.VMEM((nchunk, nrow * SLOT, TL), F32),
            pltpu.VMEM((nchunk, nrow, SLOT, TL), F32),
            pltpu.VMEM((nchunk, nrow, SLOT, TL), F32),
            pltpu.VMEM((nchunk, nrow * SLOT, TL), F32),
            pltpu.VMEM((RL * 8, TL), F32),
            pltpu.VMEM((nth, 8, TL), F32),
            pltpu.VMEM((nth, 8, TL), F32),
            pltpu.VMEM((nth * 8, TL), F32),
            dma((nchunk,)), dma((nchunk,)), dma((nchunk,)), dma((nchunk,)), dma((nchunk,)),
            dma, dma, dma, dma, dma,
        ],
        compiler_params=pltpu.CompilerParams(
            collective_id=0, has_side_effects=True, vmem_limit_bytes=58 * 1024 * 1024
        ),
        name="solve",
    )(rhs.reshape(V, K * RL, TL), jnp.swapaxes(dr, 0, 1), jnp.swapaxes(dt, 0, 1), mixm, mixo)
    out = pl.pallas_call(
        functools.partial(finish_kernel, sizes),
        out_shape=field,
        in_specs=[vmem, vmem, vmem, vmem],
        out_specs=hbm,
        scratch_shapes=[pltpu.VMEM((V, K * RL, TL), F32), dma((K * LINE // TL,))],
        compiler_params=pltpu.CompilerParams(vmem_limit_bytes=16 * 1024 * 1024),
        name="finish",
    )(l2, infl, etab, gain)
    return out.reshape(V, K, RL, TL)


def solution(mesh):
    return jax.shard_map(
        functools.partial(body, mesh.shape["row"], mesh.shape["theta"]),
        mesh=mesh,
        in_specs=(
            P(None, None, "row", "theta"),
            P(),
            P(),
            P(None, None, None, "row"),
            P(None, None, None, "row"),
        ),
        out_specs=P(None, None, "row", "theta"),
        check_vma=False,
    )
```

```python
import functools

import jax
import jax.numpy as jnp
from jax import lax
from jax.experimental import pallas as pl
from jax.experimental.pallas import tpu as pltpu
from jax.sharding import PartitionSpec as P

MESH = pl.DeviceIdType.MESH
KC = 8
SLOT, USED = 24, 20
STATES = 4
CUT_1, CUT_2 = 0, 16
LINE = 32
F32 = jnp.float32
BF16 = jnp.bfloat16


def row_peer(me, i, n):
    half = n // 2
    step = jnp.where(i < half, i, i - half)
    shift = lax.rem(half // 2 + jnp.where(step % 2 == 0, half - step // 2, (step + 1) // 2), half)
    side = jnp.where(i < half, me // half + 1, me // half) % 2
    return side * half + lax.rem(me + shift, half)


def theta_peer(me, i, n):
    return lax.rem(me + n // 2 + jnp.where(i % 2 == 0, n - i // 2, (i + 1) // 2), n)


def gap(u):
    h = 0.5 * u
    q = h * h
    series = 1.0 + q / 6.0 * (1.0 + q / 20.0 * (1.0 + q / 42.0 * (1.0 + q / 72.0)))
    return 2.0 * jnp.exp(-h) * h * series


def split(x):
    hi = x.astype(BF16)
    return hi, (x - hi.astype(F32)).astype(BF16)


def block_transfer(u1, u2, doublings):
    a, b = jnp.exp(-u1), jnp.exp(-u2)
    c = a
    q11, q12, q21, q22 = a, b, a, b
    for _ in range(doublings):
        x11, x12 = q11 * a + q12 * c, q12 * b
        x21, x22 = q21 * a + q22 * c, q22 * b
        q11, q12, q21, q22 = (
            q11 + a * x11,
            q12 + a * x12,
            q21 + c * x11 + b * x21,
            q22 + c * x12 + b * x22,
        )
        c = c * (a + b)
        a, b = a * a, b * b
    return a, b, c, q11, q12, q21, q22


def pick_lane(values, index):
    lane = lax.broadcasted_iota(jnp.int32, values.shape, 1)
    return jnp.sum(jnp.where(lane == index, values, 0.0), axis=1, keepdims=True)


def power_tables(u1, u2, n, bits):
    nf = n.astype(F32)
    a, b = jnp.exp(-nf * u1), jnp.exp(-nf * u2)
    ab, bb = jnp.exp(-u1), jnp.exp(-u2)
    pb = jnp.ones_like(ab)
    p = jnp.zeros_like(nf * u1)
    low = jnp.ones_like(p)
    for bit in range(bits):
        has = (n >> bit) & 1 == 1
        p = jnp.where(has, ab * p + low * pb, p)
        low = jnp.where(has, low * bb, low)
        pb = pb * (ab + bb)
        ab, bb = ab * ab, bb * bb
    return a, b, p


def solve_kernel(
    sizes, rhs, decay_r, decay_t, mixm, mixo, l2, infl, etab, gain,
    xin, xbuf, zbuf, ybuf, rcoef, ucol, h0tab, h1tab, wtab, wturn, gtab, mcoef, mflat, mcat, mrows, xsplit, xt,
    e1, rcv1, o1, rcv2, tx1, trc1, tx2,
    in_sem, s1s, s1r, s2s, s2r, t1s, t1r, t2s, t2r,
):
    V, K, RL, TL, nrow, nth = sizes
    nchunk = K // KC
    me_r = lax.axis_index("row")
    me_t = lax.axis_index("theta")
    kr = KC * RL
    dr = [decay_r[:, j, :] for j in range(2)]
    dt = [decay_t[:, j, :] for j in range(2)]

    def in_copy(c):
        return pltpu.make_async_copy(rhs.at[:, pl.ds(c * kr, kr), :], xin.at[c], in_sem.at[c])

    for c in range(nchunk):
        in_copy(c).start()

    barrier = pltpu.get_barrier_semaphore()

    @pl.loop(0, nth - 1)
    def _(i):
        pl.semaphore_signal(barrier, inc=1, device_id={"theta": theta_peer(me_t, i, nth)}, device_id_type=MESH)

    @pl.loop(0, nrow - 1)
    def _(i):
        pl.semaphore_signal(barrier, inc=1, device_id={"row": row_peer(me_r, i, nrow)}, device_id_type=MESH)

    cells_r = RL * nrow
    ur1, ur2 = dr[0] / cells_r, dr[1] / cells_r
    fr = gap(ur1) * gap(ur2)
    diag = lax.broadcasted_iota(jnp.int32, (K, K), 0) == lax.broadcasted_iota(jnp.int32, (K, K), 1)

    def to_columns(table, ref, j):
        for m in range(V):
            column = jnp.sum(
                jnp.where(diag, jnp.broadcast_to(table[m : m + 1, :], (K, K)), 0.0), axis=1, keepdims=True
            )
            ref[j, m] = jnp.broadcast_to(column, (K, TL))

    for j, table in enumerate((jnp.exp(-ur1), jnp.exp(-ur2), fr * fr)):
        to_columns(table, rcoef, j)
    radial_block = block_transfer(ur1, ur2, RL.bit_length() - 1)

    def radial_pass(c, states, emit):
        r1 = [rcoef[0, m, pl.ds(c * KC, KC), :] for m in range(V)]
        r2 = [rcoef[1, m, pl.ds(c * KC, KC), :] for m in range(V)]

        def ahead(r, carry):
            out = []
            for m in range(V):
                s1, s2 = carry[m]
                s1 = r1[m] * s1 + xt[c, m, pl.ds(pl.multiple_of(r * KC, KC), KC), :]
                s2 = r2[m] * s2 + s1
                ybuf[m, pl.ds(pl.multiple_of(r * KC, KC), KC), :] = s2
                out.append((s1, s2))
            return tuple(out)

        def behind(i, carry):
            r = RL - 1 - i
            out = []
            for m in range(V):
                u1, u2 = carry[m]
                u1 = r1[m] * u1 + ybuf[m, pl.ds(pl.multiple_of(r * KC, KC), KC), :]
                u2 = r2[m] * u2 + u1
                out.append((u1, u2))
            if emit is not None:
                emit(r, [pair[1] for pair in out])
            return tuple(out)

        first = lax.fori_loop(0, RL, ahead, tuple((s[0], s[1]) for s in states), unroll=8)
        second = lax.fori_loop(0, RL, behind, tuple((s[2], s[3]) for s in states), unroll=8)
        return first, second

    @pl.loop(0, nchunk)
    def _(c):
        in_copy(c).wait()

        @pl.loop(0, V)
        def _(m):
            for kk in range(KC):
                for q in range(RL // 8):
                    first_row = kk * RL + q * 8
                    xt[c, m, pl.ds(q * 8 * KC + kk, 8, stride=KC), :] = xin[c, m, first_row : first_row + 8, :]

        zero = jnp.zeros((KC, TL), F32)
        first, second = radial_pass(c, [(zero,) * 4] * V, None)
        for m in range(V):
            for s, value in enumerate((first[m][0], first[m][1], second[m][0], second[m][1])):
                e1[c, pl.ds(s * V + m, KC, stride=SLOT), :] = value

    pl.semaphore_wait(barrier, nrow - 1 + nth - 1)

    @pl.loop(0, nchunk)
    def _(c):
        @pl.loop(0, nrow - 1)
        def _(i):
            p = row_peer(me_r, i, nrow)
            pltpu.make_async_remote_copy(
                src_ref=e1.at[c, pl.ds(pl.multiple_of(p * SLOT, 8), USED), :],
                dst_ref=rcv1.at[c, me_r, pl.ds(0, USED), :],
                send_sem=s1s.at[c],
                recv_sem=s1r.at[c],
                device_id={"row": p},
                device_id_type=MESH,
            ).start()

        pltpu.make_async_copy(
            e1.at[c, pl.ds(pl.multiple_of(me_r * SLOT, 8), USED), :], rcv1.at[c, me_r, pl.ds(0, USED), :], s1r.at[c]
        ).start()

    cells_t = TL * nth
    ut1, ut2 = dt[0] / cells_t, dt[1] / cells_t
    to_columns(ut1, ucol, 0)
    to_columns(ut2, ucol, 1)
    lane32 = lax.broadcasted_iota(jnp.int32, (RL, TL), 1)
    lane8 = lax.broadcasted_iota(jnp.int32, (8, TL), 1)
    bits = TL.bit_length() - 1
    etab[...] = jnp.zeros_like(etab)
    wtab[...] = jnp.zeros_like(wtab)

    def tables(q, carry):
        m, c = q // nchunk, q % nchunk
        rows = pl.ds(pl.multiple_of(c * KC, KC), KC)
        u1, u2 = ucol[0, m, rows, :], ucol[1, m, rows, :]
        r1, r2 = jnp.exp(-u1), jnp.exp(-u2)
        f = gap(u1) * gap(u2)
        i12, i11, i22 = 1.0 / gap(u1 + u2), 1.0 / gap(2.0 * u1), 1.0 / gap(2.0 * u2)
        scale_1 = f * f * r1 * i12
        coef_a = scale_1 * i12 * (r1 * i11 + r2 * i22)
        coef_p = scale_1 * i22
        coef_b = f * f * i12 * i22
        af, bf, pf = power_tables(u1, u2, lane8, bits)
        ar, br, pr = power_tables(u1, u2, TL - 1 - lane8, bits)
        pf1, pr1 = r1 * pf + bf, r1 * pr + br
        e_t1 = coef_a * (r1 * ar) + coef_p * pr1
        e_t2 = coef_b * (r2 * br)
        h0tab[m, rows, :] = coef_a * af + coef_p * pf + coef_b * bf
        h1tab[m, rows, :] = e_t1 + e_t2
        e_s1 = coef_a * (r1 * af) + coef_p * pf1
        e_s2 = coef_b * (r2 * bf)
        for s, value in enumerate((e_s1, e_s2, e_t1, e_t2)):
            etab[pl.ds(c * KC * 32 + 8 * s + m, KC, stride=32), :] = value
        for s, value in enumerate((ar, pr1, af, pf1)):
            wtab[pl.ds(c * KC * 32 + 8 * s + m, KC, stride=32), :] = value
        return carry

    lax.fori_loop(0, V * nchunk, tables, 0, unroll=2)

    tile = TL // LINE
    for j in range(K // tile):
        hi, lo = split(wtab[j * TL : (j + 1) * TL, :].T)
        wturn[j] = jnp.concatenate(
            [jnp.concatenate([hi, hi], axis=0), jnp.concatenate([lo, jnp.zeros_like(lo)], axis=0)], axis=1
        )

    hi, lo = split(mixm.reshape(V * V * K, RL)[...])
    halves = jnp.concatenate([hi, lo], axis=1)
    pick_row = lax.broadcasted_iota(jnp.int32, (2 * RL, 2 * TL), 0) % RL
    pick_half = lax.broadcasted_iota(jnp.int32, (2 * RL, 2 * TL), 1) // TL

    @pl.loop(0, RL // 2)
    def _(i):
        pick = jnp.where(pick_row == 2 * i + pick_half, 1.0, 0.0).astype(BF16)
        both = jnp.dot(halves, pick, preferred_element_type=F32)
        mcoef[2 * i] = both[:, 0:TL]
        mcoef[2 * i + 1] = both[:, TL : 2 * TL]

    for m in range(V):
        four = jnp.concatenate([mixo[m * V + n] for n in range(V - 1)], axis=1)
        last = mixo[m * V + V - 1]
        four_hi = four.astype(BF16).astype(F32)
        last_hi = last.astype(BF16).astype(F32)
        last = jnp.concatenate([last_hi, last_hi, last - last_hi, jnp.zeros_like(last)], axis=1)
        mflat[m] = jnp.concatenate([four_hi, four - four_hi, last], axis=1)

    @pl.loop(0, K)
    def _(k):
        for m in range(V):
            mcat[k, m] = jnp.broadcast_to(mflat[m, pl.ds(k, 1), :], (16, 3 * TL)).astype(BF16)

    row16 = lax.broadcasted_iota(jnp.int32, (16, 3 * TL), 0)
    col16 = lax.broadcasted_iota(jnp.int32, (16, 3 * TL), 1) % RL
    on_diagonal = [jnp.where(row16 + 16 * half == col16, 1.0, 0.0).astype(BF16) for half in range(RL // 16)]

    def mix(k, field):
        hi, lo = split(field)
        four = (V - 1) * RL
        right = jnp.concatenate(
            [hi[0:four], lo[0:four], hi[0:four], hi[four:], lo[four:], hi[four:], jnp.zeros((RL, TL), BF16)], axis=0
        )
        left = jnp.concatenate([mcat[k, m] * mask for m in range(V) for mask in on_diagonal], axis=0)
        left = jnp.concatenate([left[:, 0:TL], left], axis=1)
        return jnp.dot(left, right, preferred_element_type=F32)

    lane16 = lax.broadcasted_iota(jnp.int32, (16, TL), 1)
    sub16 = lax.broadcasted_iota(jnp.int32, (16, TL), 0)

    def toeplitz(k):
        for m in range(V):
            near = pltpu.roll(jnp.broadcast_to(h0tab[m, pl.ds(k, 1), :], (16, TL)), 0, 1, stride=1, stride_axis=0)
            far = pltpu.roll(jnp.broadcast_to(h1tab[m, pl.ds(k, 1), :], (16, TL)), 0, 1, stride=1, stride_axis=0)
            near = jnp.where(lane16 < sub16, far, near)
            for part, (n, f) in enumerate(zip(split(near), split(far))):
                for b in range(TL // 16):
                    rows = pltpu.roll(jnp.where(lane16 >= TL - 16 * b, f, n), 16 * b, 1) if b else n
                    gtab[k, m, 16 * b : 16 * b + 16, part * TL : part * TL + TL] = rows

    def some_toeplitz(first, last):
        @pl.loop(first, last)
        def _(k):
            toeplitz(k)

    some_toeplitz(0, CUT_1)

    @pl.loop(0, nchunk)
    def _(c):
        a, b, cc, q11, q12, q21, q22 = (
            jnp.broadcast_to(pick_lane(x, c * KC + me_r), (V, TL)) for x in radial_block
        )
        arrived = rcv1.at[c, :, pl.ds(0, USED), :]
        pltpu.make_async_copy(arrived, arrived, s1r.at[c]).wait()

        def got(d, s):
            return rcv1[c, d, s * V : s * V + V, :]

        zero = jnp.zeros((V, TL), F32)
        sa, sb = [zero], [zero]
        for d in range(nrow - 1):
            sa.append(a * sa[d] + got(d, 0))
            sb.append(b * sb[d] + cc * sa[d] + got(d, 1))
        ta, tb = zero, zero
        for d in range(nrow - 1, -1, -1):
            for s, value in enumerate((sa[d], sb[d], ta, tb)):
                o1[c, d, s * V : s * V + V, :] = value
            if d:
                ta, tb = (
                    a * ta + got(d, 2) + q11 * sa[d] + q12 * sb[d],
                    b * tb + cc * ta + got(d, 3) + q21 * sa[d] + q22 * sb[d],
                )

        @pl.loop(0, nrow - 1)
        def _(i):
            p = row_peer(me_r, i, nrow)
            pltpu.make_async_remote_copy(
                src_ref=o1.at[c, p, pl.ds(0, USED), :],
                dst_ref=rcv2.at[c, pl.ds(pl.multiple_of(me_r * SLOT, 8), USED), :],
                send_sem=s2s.at[c],
                recv_sem=s2r.at[c],
                device_id={"row": p},
                device_id_type=MESH,
            ).start()

        pltpu.make_async_copy(
            o1.at[c, me_r, pl.ds(0, USED), :], rcv2.at[c, pl.ds(pl.multiple_of(me_r * SLOT, 8), USED), :], s2r.at[c]
        ).start()

    some_toeplitz(CUT_1, CUT_2)

    @pl.loop(0, nchunk)
    def _(c):
        arrived = rcv2.at[c, pl.ds(0, nrow * USED), :]
        pltpu.make_async_copy(arrived, arrived, s2r.at[c]).wait()
        states = [
            tuple(rcv2[c, pl.ds(s * V + m, KC, stride=SLOT), :] for s in range(4)) for m in range(V)
        ]
        f2 = [rcoef[2, m, pl.ds(c * KC, KC), :] for m in range(V)]

        def emit(r, z):
            z = [f2[m] * z[m] for m in range(V)]
            for m in range(V):
                total = None
                for n in range(V):
                    term = mcoef[r, pl.ds(pl.multiple_of((m * V + n) * K + c * KC, KC), KC), :] * z[n]
                    total = term if total is None else total + term
                xbuf[m, pl.ds(pl.multiple_of(r * KC, KC), KC), :] = total

        radial_pass(c, states, emit)

        def leaving(j, carry):
            total = jnp.zeros((RL, TL), F32)
            for kk in range(tile):
                k = c * KC + j * tile + kk
                field = [xbuf[m, pl.ds(j * tile + kk, RL, stride=KC), :] for m in range(V)]
                hi, lo = split(jnp.concatenate(field, axis=0))
                xsplit[k, :, 0:TL] = hi
                xsplit[k, :, TL : 2 * TL] = lo
                out = jnp.dot(
                    jnp.concatenate([hi, lo], axis=1), wturn[c * (KC // tile) + j], preferred_element_type=F32
                )
                out = out[:, 0:TL] + out[:, TL : 2 * TL]
                for m in range(V):
                    mine = (lane32 // LINE == kk) & (lane32 % 8 == m)
                    total = total + jnp.where(mine, out[m * RL : m * RL + RL], 0.0)
            tx1[pl.ds(c * (KC // tile) + j, RL, stride=8), :] = total
            return carry

        lax.fori_loop(0, KC // tile, leaving, 0, unroll=True)

    @pl.loop(0, nth - 1)
    def _(i):
        p = theta_peer(me_t, i, nth)
        pltpu.make_async_remote_copy(
            src_ref=tx1.at[pl.ds(pl.multiple_of(p * 8, 8), 8), :],
            dst_ref=trc1.at[me_t],
            send_sem=t1s,
            recv_sem=t1r,
            device_id={"theta": p},
            device_id_type=MESH,
        ).start()

    pltpu.make_async_copy(tx1.at[pl.ds(pl.multiple_of(me_t * 8, 8), 8), :], trc1.at[me_t], t1r).start()

    def local_solve(c):
        def solve(kk, carry):
            k = c * KC + kk
            for m in range(V):
                hi = xsplit[k, m * RL : m * RL + RL, 0:TL]
                lo = xsplit[k, m * RL : m * RL + RL, TL : 2 * TL]
                z = jnp.dot(jnp.concatenate([hi, lo], axis=0), gtab[k, m], preferred_element_type=F32)
                z = z[0:RL, 0:TL] + z[RL : 2 * RL, 0:TL] + z[0:RL, TL : 2 * TL]
                zbuf[m, pl.ds(pl.multiple_of(kk * RL, RL), RL), :] = z
            return carry

        lax.fori_loop(0, KC, solve, 0, unroll=4)

        def out_mix(kk, carry):
            rows = pl.ds(pl.multiple_of(kk * RL, RL), RL)
            field = mix(c * KC + kk, jnp.concatenate([zbuf[n, rows, :] for n in range(V)], axis=0))
            for m in range(V):
                l2[m, pl.ds(pl.multiple_of((c * KC + kk) * RL, RL), RL), :] = field[m * RL : m * RL + RL]
            return carry

        lax.fori_loop(0, KC, out_mix, 0, unroll=4)

    mrows[...] = jnp.zeros_like(mrows)
    for m in range(V):
        for n in range(V):
            mrows[pl.ds(m * K * 8 + n, K, stride=8), 0:RL] = mixo[m * V + n]
    group = 8 * TL // LINE
    source = lax.broadcasted_iota(jnp.int32, (TL, TL), 0)
    target = lax.broadcasted_iota(jnp.int32, (TL, TL), 1)
    source_rows = 8 * (target // LINE) + target % 8
    turned = []
    for m in range(V):
        for j in range(K * 8 // TL):
            turned.append(mrows[pl.ds(m * K * 8 + j * TL, TL), :].T[0:RL])
    hi, lo = split(jnp.concatenate(turned, axis=0))
    halves = jnp.concatenate([hi, lo], axis=1)
    for q in range(TL // group):
        pick = jnp.where(source == source_rows + q * group, 1.0, 0.0).astype(BF16)
        spread_rows = jnp.dot(halves, jnp.concatenate([pick, pick], axis=0), preferred_element_type=F32)
        for m in range(V):
            for j in range(K * 8 // TL):
                i = m * (K * 8 // TL) + j
                gain[j * (TL // group) + q, m * RL : m * RL + RL, :] = spread_rows[i * RL : i * RL + RL]

    some_toeplitz(CUT_2, K)
    local_solve(0)

    u1, u2 = jnp.ones((8, TL), F32), jnp.ones((8, TL), F32)
    for kk in range(tile):
        for m in range(V):
            mine = (lane8 // LINE == kk) & (lane8 % 8 == m)
            u1 = jnp.where(mine, ucol[0, m, pl.ds(kk, 8, stride=tile), :], u1)
            u2 = jnp.where(mine, ucol[1, m, pl.ds(kk, 8, stride=tile), :], u2)
    a, b, cc = block_transfer(u1, u2, bits)[:3]
    around_1 = 1.0 / (1.0 - jnp.exp(-cells_t * u1))
    around_2 = 1.0 / (1.0 - jnp.exp(-cells_t * u2))
    pltpu.make_async_copy(trc1, trc1, t1r).wait()
    forward = lane8 % LINE < LINE // 2
    entering = [jnp.where(forward, trc1[i], trc1[nth - 1 - i]) for i in range(nth)]

    def cycle(rate, decay, around, terms):
        chain = [jnp.zeros((8, TL), F32)]
        for i in range(nth):
            chain.append(rate * chain[i] + terms[i])
        start = chain[nth] * around
        return [chain[i] + jnp.exp(-(TL * i) * decay) * start for i in range(nth)]

    one = cycle(a, u1, around_1, entering)
    two = cycle(b, u2, around_2, [entering[i] + cc * pltpu.roll(one[i], 8, 1) for i in range(nth)])
    even = lane8 // 8 % 2 == 0
    state = [jnp.where(even, one[i], two[i]) for i in range(nth)]
    for d in range(nth):
        tx2[d] = jnp.where(forward, state[d], state[nth - 1 - d])

    @pl.loop(0, nth - 1)
    def _(i):
        d = theta_peer(me_t, i, nth)
        pltpu.make_async_remote_copy(
            src_ref=tx2.at[d],
            dst_ref=infl.at[pl.ds(pl.multiple_of(me_t * 8, 8), 8), :],
            send_sem=t2s,
            recv_sem=t2r,
            device_id={"theta": d},
            device_id_type=MESH,
        ).start()

    pltpu.make_async_copy(tx2.at[me_t], infl.at[pl.ds(pl.multiple_of(me_t * 8, 8), 8), :], t2r).start()

    @pl.loop(1, nchunk)
    def _(c):
        local_solve(c)

    pltpu.make_async_copy(infl, infl, t2r).wait()

    @pl.loop(0, nchunk)
    def _(c):
        sent = rcv1.at[c, pl.ds(0, nrow - 1), pl.ds(0, USED), :]
        pltpu.make_async_copy(sent, sent, s1s.at[c]).wait()
        pltpu.make_async_copy(sent, sent, s2s.at[c]).wait()

    sent = trc1.at[pl.ds(0, nth - 1)]
    pltpu.make_async_copy(sent, sent, t1s).wait()
    pltpu.make_async_copy(sent, sent, t2s).wait()


def finish_kernel(sizes, l2, infl, etab, gain, out, buf, sem):
    V, K, RL, TL, nrow, nth = sizes
    tile = TL // LINE
    kr = tile * RL
    row = lax.broadcasted_iota(jnp.int32, (TL, TL), 0) // LINE

    def out_copy(j):
        rows = pl.ds(pl.multiple_of(j * kr, kr), kr)
        return pltpu.make_async_copy(buf.at[:, rows, :], out.at[:, rows, :], sem.at[j])

    @pl.loop(0, K // tile)
    def _(j):
        state = infl[pl.ds(j, RL, stride=8), :]
        hi, lo = split(gain[j] * jnp.concatenate([state] * V, axis=0))
        left = jnp.concatenate([hi, lo], axis=1)
        response = etab[pl.ds(pl.multiple_of(j * TL, TL), TL), :]
        for kk in range(tile):
            ehi, elo = split(jnp.where(row == kk, response, 0.0))
            right = jnp.concatenate(
                [jnp.concatenate([ehi, ehi], axis=0), jnp.concatenate([elo, jnp.zeros_like(elo)], axis=0)], axis=1
            )
            inflow = jnp.dot(left, right, preferred_element_type=F32)
            inflow = inflow[:, 0:TL] + inflow[:, TL : 2 * TL]
            rows = pl.ds(pl.multiple_of(j * kr + kk * RL, RL), RL)
            for m in range(V):
                buf[m, rows, :] = l2[m, rows, :] + inflow[m * RL : m * RL + RL]
        out_copy(j).start()

    @pl.loop(0, K // tile)
    def _(j):
        out_copy(j).wait()


def body(nrow, nth, rhs, dr, dt, mixm, mixo):
    V, K, RL, TL = rhs.shape
    sizes = (V, K, RL, TL, nrow, nth)
    nchunk = K // KC
    kr = KC * RL
    field = jax.ShapeDtypeStruct((V, K * RL, TL), F32)
    vmem = pl.BlockSpec(memory_space=pltpu.VMEM)
    hbm = pl.BlockSpec(memory_space=pl.ANY)
    mixm = mixm.reshape(V * V, K, RL)
    mixo = mixo.reshape(V * V, K, RL)
    dma = pltpu.SemaphoreType.DMA
    nline = K * LINE // TL
    l2, infl, etab, gain = pl.pallas_call(
        functools.partial(solve_kernel, sizes),
        out_shape=(
            pltpu.VMEM((V, K * RL, TL), F32),
            pltpu.VMEM((nth * 8, TL), F32),
            pltpu.VMEM((K * LINE, TL), F32),
            pltpu.VMEM((nline, V * RL, TL), F32),
        ),
        in_specs=[pl.BlockSpec(memory_space=pltpu.HBM), vmem, vmem, vmem, vmem],
        out_specs=(vmem, vmem, vmem, vmem),
        scratch_shapes=[
            pltpu.VMEM((nchunk, V, kr, TL), F32),
            pltpu.VMEM((V, kr, TL), F32),
            pltpu.VMEM((V, kr, TL), F32),
            pltpu.VMEM((V, kr, TL), F32),
            pltpu.VMEM((3, V, K, TL), F32),
            pltpu.VMEM((2, V, K, TL), F32),
            pltpu.VMEM((V, K, TL), F32),
            pltpu.VMEM((V, K, TL), F32),
            pltpu.VMEM((K * LINE, TL), F32),
            pltpu.VMEM((nline, 2 * TL, 2 * TL), BF16),
            pltpu.VMEM((K, V, TL, 2 * TL), BF16),
            pltpu.VMEM((RL, V * V * K, TL), F32),
            pltpu.VMEM((V, K, 3 * TL), F32),
            pltpu.VMEM((K, V, 16, 3 * TL), BF16),
            pltpu.VMEM((V * K * 8, TL), F32),
            pltpu.VMEM((K, V * RL, 2 * TL), BF16),
            pltpu.VMEM((nchunk, V, kr, TL), F32),
            pltpu.VMEM((nchunk, nrow * SLOT, TL), F32),
            pltpu.VMEM((nchunk, nrow, SLOT, TL), F32),
            pltpu.VMEM((nchunk, nrow, SLOT, TL), F32),
            pltpu.VMEM((nchunk, nrow * SLOT, TL), F32),
            pltpu.VMEM((RL * 8, TL), F32),
            pltpu.VMEM((nth, 8, TL), F32),
            pltpu.VMEM((nth, 8, TL), F32),
            dma((nchunk,)), dma((nchunk,)), dma((nchunk,)), dma((nchunk,)), dma((nchunk,)),
            dma, dma, dma, dma,
        ],
        compiler_params=pltpu.CompilerParams(
            collective_id=0, has_side_effects=True, vmem_limit_bytes=58 * 1024 * 1024
        ),
        name="solve",
    )(rhs.reshape(V, K * RL, TL), jnp.swapaxes(dr, 0, 1), jnp.swapaxes(dt, 0, 1), mixm, mixo)
    out = pl.pallas_call(
        functools.partial(finish_kernel, sizes),
        out_shape=field,
        in_specs=[vmem, vmem, vmem, vmem],
        out_specs=hbm,
        scratch_shapes=[pltpu.VMEM((V, K * RL, TL), F32), dma((K * LINE // TL,))],
        compiler_params=pltpu.CompilerParams(vmem_limit_bytes=16 * 1024 * 1024),
        name="finish",
    )(l2, infl, etab, gain)
    return out.reshape(V, K, RL, TL)


def solution(mesh):
    return jax.shard_map(
        functools.partial(body, mesh.shape["row"], mesh.shape["theta"]),
        mesh=mesh,
        in_specs=(
            P(None, None, "row", "theta"),
            P(),
            P(),
            P(None, None, None, "row"),
            P(None, None, None, "row"),
        ),
        out_specs=P(None, None, "row", "theta"),
        check_vma=False,
    )
```

```python
import functools

import jax
import jax.numpy as jnp
from jax import lax
from jax.experimental import pallas as pl
from jax.experimental.pallas import tpu as pltpu
from jax.sharding import PartitionSpec as P

MESH = pl.DeviceIdType.MESH
KC = 8
SLOT, USED = 24, 20
STATES = 4
CUT_2 = 12
LINE = 32
F32 = jnp.float32
BF16 = jnp.bfloat16


def row_peer(me, i, n):
    half = n // 2
    step = jnp.where(i < half, i, i - half)
    shift = lax.rem(half // 2 + jnp.where(step % 2 == 0, half - step // 2, (step + 1) // 2), half)
    side = jnp.where(i < half, me // half + 1, me // half) % 2
    return side * half + lax.rem(me + shift, half)


def theta_peer(me, i, n):
    return lax.rem(me + n // 2 + jnp.where(i % 2 == 0, n - i // 2, (i + 1) // 2), n)


def gap(u):
    h = 0.5 * u
    q = h * h
    series = 1.0 + q / 6.0 * (1.0 + q / 20.0 * (1.0 + q / 42.0 * (1.0 + q / 72.0)))
    return 2.0 * jnp.exp(-h) * h * series


def split(x):
    hi = x.astype(BF16)
    return hi, (x - hi.astype(F32)).astype(BF16)


def block_transfer(u1, u2, doublings):
    a, b = jnp.exp(-u1), jnp.exp(-u2)
    c = a
    q11, q12, q21, q22 = a, b, a, b
    for _ in range(doublings):
        x11, x12 = q11 * a + q12 * c, q12 * b
        x21, x22 = q21 * a + q22 * c, q22 * b
        q11, q12, q21, q22 = (
            q11 + a * x11,
            q12 + a * x12,
            q21 + c * x11 + b * x21,
            q22 + c * x12 + b * x22,
        )
        c = c * (a + b)
        a, b = a * a, b * b
    return a, b, c, q11, q12, q21, q22


def pick_lane(values, index):
    lane = lax.broadcasted_iota(jnp.int32, values.shape, 1)
    return jnp.sum(jnp.where(lane == index, values, 0.0), axis=1, keepdims=True)


def power_tables(u1, u2, n, bits):
    nf = n.astype(F32)
    a, b = jnp.exp(-nf * u1), jnp.exp(-nf * u2)
    ab, bb = jnp.exp(-u1), jnp.exp(-u2)
    pb = jnp.ones_like(ab)
    p = jnp.zeros_like(nf * u1)
    low = jnp.ones_like(p)
    for bit in range(bits):
        has = (n >> bit) & 1 == 1
        p = jnp.where(has, ab * p + low * pb, p)
        low = jnp.where(has, low * bb, low)
        pb = pb * (ab + bb)
        ab, bb = ab * ab, bb * bb
    return a, b, p


def solve_kernel(
    sizes, rhs, decay_r, decay_t, mixm, mixo, l2, infl, etab, gain,
    xin, xbuf, zbuf, ybuf, rcoef, ucol, h0tab, h1tab, wtab, wturn, gtab, mcoef, mflat, mcat, mrows, xsplit, xt,
    e1, rcv1, o1, rcv2, tx1, trc1, tx2,
    in_sem, s1s, s1r, s2s, s2r, t1s, t1r, t2s, t2r,
):
    V, K, RL, TL, nrow, nth = sizes
    nchunk = K // KC
    me_r = lax.axis_index("row")
    me_t = lax.axis_index("theta")
    kr = KC * RL
    dr = [decay_r[:, j, :] for j in range(2)]
    dt = [decay_t[:, j, :] for j in range(2)]

    def in_copy(c):
        return pltpu.make_async_copy(rhs.at[:, pl.ds(c * kr, kr), :], xin.at[c], in_sem.at[c])

    for c in range(nchunk):
        in_copy(c).start()

    barrier = pltpu.get_barrier_semaphore()

    @pl.loop(0, nth - 1)
    def _(i):
        pl.semaphore_signal(barrier, inc=1, device_id={"theta": theta_peer(me_t, i, nth)}, device_id_type=MESH)

    @pl.loop(0, nrow - 1)
    def _(i):
        pl.semaphore_signal(barrier, inc=1, device_id={"row": row_peer(me_r, i, nrow)}, device_id_type=MESH)

    cells_r = RL * nrow
    ur1, ur2 = dr[0] / cells_r, dr[1] / cells_r
    fr = gap(ur1) * gap(ur2)
    diag = lax.broadcasted_iota(jnp.int32, (K, K), 0) == lax.broadcasted_iota(jnp.int32, (K, K), 1)

    def to_columns(table, ref, j):
        for m in range(V):
            column = jnp.sum(
                jnp.where(diag, jnp.broadcast_to(table[m : m + 1, :], (K, K)), 0.0), axis=1, keepdims=True
            )
            ref[j, m] = jnp.broadcast_to(column, (K, TL))

    for j, table in enumerate((jnp.exp(-ur1), jnp.exp(-ur2), fr * fr)):
        to_columns(table, rcoef, j)
    radial_block = block_transfer(ur1, ur2, RL.bit_length() - 1)

    def radial_pass(c, states, emit):
        r1 = [rcoef[0, m, pl.ds(c * KC, KC), :] for m in range(V)]
        r2 = [rcoef[1, m, pl.ds(c * KC, KC), :] for m in range(V)]

        def ahead(r, carry):
            out = []
            for m in range(V):
                s1, s2 = carry[m]
                s1 = r1[m] * s1 + xt[c, m, pl.ds(pl.multiple_of(r * KC, KC), KC), :]
                s2 = r2[m] * s2 + s1
                ybuf[m, pl.ds(pl.multiple_of(r * KC, KC), KC), :] = s2
                out.append((s1, s2))
            return tuple(out)

        def behind(i, carry):
            r = RL - 1 - i
            out = []
            for m in range(V):
                u1, u2 = carry[m]
                u1 = r1[m] * u1 + ybuf[m, pl.ds(pl.multiple_of(r * KC, KC), KC), :]
                u2 = r2[m] * u2 + u1
                out.append((u1, u2))
            if emit is not None:
                emit(r, [pair[1] for pair in out])
            return tuple(out)

        first = lax.fori_loop(0, RL, ahead, tuple((s[0], s[1]) for s in states), unroll=8)
        second = lax.fori_loop(0, RL, behind, tuple((s[2], s[3]) for s in states), unroll=8)
        return first, second

    @pl.loop(0, nchunk)
    def _(c):
        in_copy(c).wait()

        @pl.loop(0, V)
        def _(m):
            for kk in range(KC):
                for q in range(RL // 8):
                    first_row = kk * RL + q * 8
                    xt[c, m, pl.ds(q * 8 * KC + kk, 8, stride=KC), :] = xin[c, m, first_row : first_row + 8, :]

        zero = jnp.zeros((KC, TL), F32)
        first, second = radial_pass(c, [(zero,) * 4] * V, None)
        for m in range(V):
            for s, value in enumerate((first[m][0], first[m][1], second[m][0], second[m][1])):
                e1[c, pl.ds(s * V + m, KC, stride=SLOT), :] = value

    pl.semaphore_wait(barrier, nrow - 1 + nth - 1)

    @pl.loop(0, nchunk)
    def _(c):
        @pl.loop(0, nrow - 1)
        def _(i):
            p = row_peer(me_r, i, nrow)
            pltpu.make_async_remote_copy(
                src_ref=e1.at[c, pl.ds(pl.multiple_of(p * SLOT, 8), USED), :],
                dst_ref=rcv1.at[c, me_r, pl.ds(0, USED), :],
                send_sem=s1s.at[c],
                recv_sem=s1r.at[c],
                device_id={"row": p},
                device_id_type=MESH,
            ).start()

        pltpu.make_async_copy(
            e1.at[c, pl.ds(pl.multiple_of(me_r * SLOT, 8), USED), :], rcv1.at[c, me_r, pl.ds(0, USED), :], s1r.at[c]
        ).start()

    cells_t = TL * nth
    ut1, ut2 = dt[0] / cells_t, dt[1] / cells_t
    to_columns(ut1, ucol, 0)
    to_columns(ut2, ucol, 1)
    lane32 = lax.broadcasted_iota(jnp.int32, (RL, TL), 1)
    lane8 = lax.broadcasted_iota(jnp.int32, (8, TL), 1)
    bits = TL.bit_length() - 1
    etab[...] = jnp.zeros_like(etab)
    wtab[...] = jnp.zeros_like(wtab)

    def tables(q, carry):
        m, c = q // nchunk, q % nchunk
        rows = pl.ds(pl.multiple_of(c * KC, KC), KC)
        u1, u2 = ucol[0, m, rows, :], ucol[1, m, rows, :]
        r1, r2 = jnp.exp(-u1), jnp.exp(-u2)
        f = gap(u1) * gap(u2)
        i12, i11, i22 = 1.0 / gap(u1 + u2), 1.0 / gap(2.0 * u1), 1.0 / gap(2.0 * u2)
        scale_1 = f * f * r1 * i12
        coef_a = scale_1 * i12 * (r1 * i11 + r2 * i22)
        coef_p = scale_1 * i22
        coef_b = f * f * i12 * i22
        af, bf, pf = power_tables(u1, u2, lane8, bits)
        ar, br, pr = power_tables(u1, u2, TL - 1 - lane8, bits)
        pf1, pr1 = r1 * pf + bf, r1 * pr + br
        e_t1 = coef_a * (r1 * ar) + coef_p * pr1
        e_t2 = coef_b * (r2 * br)
        h0tab[m, rows, :] = coef_a * af + coef_p * pf + coef_b * bf
        h1tab[m, rows, :] = e_t1 + e_t2
        e_s1 = coef_a * (r1 * af) + coef_p * pf1
        e_s2 = coef_b * (r2 * bf)
        for s, value in enumerate((e_s1, e_s2, e_t1, e_t2)):
            etab[pl.ds(c * KC * 32 + 8 * s + m, KC, stride=32), :] = value
        for s, value in enumerate((ar, pr1, af, pf1)):
            wtab[pl.ds(c * KC * 32 + 8 * s + m, KC, stride=32), :] = value
        return carry

    lax.fori_loop(0, V * nchunk, tables, 0, unroll=2)

    tile = TL // LINE
    for j in range(K // tile):
        hi, lo = split(wtab[j * TL : (j + 1) * TL, :].T)
        wturn[j] = jnp.concatenate(
            [jnp.concatenate([hi, hi], axis=0), jnp.concatenate([lo, jnp.zeros_like(lo)], axis=0)], axis=1
        )

    hi, lo = split(mixm.reshape(V * V * K, RL)[...])
    halves = jnp.concatenate([hi, lo], axis=1)
    pick_row = lax.broadcasted_iota(jnp.int32, (2 * RL, 2 * TL), 0) % RL
    pick_half = lax.broadcasted_iota(jnp.int32, (2 * RL, 2 * TL), 1) // TL

    @pl.loop(0, RL // 2)
    def _(i):
        pick = jnp.where(pick_row == 2 * i + pick_half, 1.0, 0.0).astype(BF16)
        both = jnp.dot(halves, pick, preferred_element_type=F32)
        mcoef[2 * i] = both[:, 0:TL]
        mcoef[2 * i + 1] = both[:, TL : 2 * TL]

    row16 = lax.broadcasted_iota(jnp.int32, (16, 3 * TL), 0)
    col16 = lax.broadcasted_iota(jnp.int32, (16, 3 * TL), 1) % RL
    on_diagonal = [jnp.where(row16 + 16 * half == col16, 1.0, 0.0).astype(BF16) for half in range(RL // 16)]

    def mix(k, field):
        hi, lo = split(field)
        four = (V - 1) * RL
        right = jnp.concatenate(
            [hi[0:four], lo[0:four], hi[0:four], hi[four:], lo[four:], hi[four:], jnp.zeros((RL, TL), BF16)], axis=0
        )
        left = jnp.concatenate([mcat[k, m] * mask for m in range(V) for mask in on_diagonal], axis=0)
        left = jnp.concatenate([left[:, 0:TL], left], axis=1)
        return jnp.dot(left, right, preferred_element_type=F32)

    lane16 = lax.broadcasted_iota(jnp.int32, (16, TL), 1)
    sub16 = lax.broadcasted_iota(jnp.int32, (16, TL), 0)

    def toeplitz(k):
        for m in range(V):
            near = pltpu.roll(jnp.broadcast_to(h0tab[m, pl.ds(k, 1), :], (16, TL)), 0, 1, stride=1, stride_axis=0)
            far = pltpu.roll(jnp.broadcast_to(h1tab[m, pl.ds(k, 1), :], (16, TL)), 0, 1, stride=1, stride_axis=0)
            near = jnp.where(lane16 < sub16, far, near)
            for part, (n, f) in enumerate(zip(split(near), split(far))):
                for b in range(TL // 16):
                    rows = pltpu.roll(jnp.where(lane16 >= TL - 16 * b, f, n), 16 * b, 1) if b else n
                    gtab[k, m, 16 * b : 16 * b + 16, part * TL : part * TL + TL] = rows

    def some_toeplitz(first, last):
        @pl.loop(first, last)
        def _(k):
            toeplitz(k)

    @pl.loop(0, nchunk)
    def _(c):
        a, b, cc, q11, q12, q21, q22 = (
            jnp.broadcast_to(pick_lane(x, c * KC + me_r), (V, TL)) for x in radial_block
        )
        arrived = rcv1.at[c, :, pl.ds(0, USED), :]
        pltpu.make_async_copy(arrived, arrived, s1r.at[c]).wait()

        def got(d, s):
            return rcv1[c, d, s * V : s * V + V, :]

        zero = jnp.zeros((V, TL), F32)
        sa, sb = [zero], [zero]
        for d in range(nrow - 1):
            sa.append(a * sa[d] + got(d, 0))
            sb.append(b * sb[d] + cc * sa[d] + got(d, 1))
        ta, tb = zero, zero
        for d in range(nrow - 1, -1, -1):
            for s, value in enumerate((sa[d], sb[d], ta, tb)):
                o1[c, d, s * V : s * V + V, :] = value
            if d:
                ta, tb = (
                    a * ta + got(d, 2) + q11 * sa[d] + q12 * sb[d],
                    b * tb + cc * ta + got(d, 3) + q21 * sa[d] + q22 * sb[d],
                )

        @pl.loop(0, nrow - 1)
        def _(i):
            p = row_peer(me_r, i, nrow)
            pltpu.make_async_remote_copy(
                src_ref=o1.at[c, p, pl.ds(0, USED), :],
                dst_ref=rcv2.at[c, pl.ds(pl.multiple_of(me_r * SLOT, 8), USED), :],
                send_sem=s2s.at[c],
                recv_sem=s2r.at[c],
                device_id={"row": p},
                device_id_type=MESH,
            ).start()

        pltpu.make_async_copy(
            o1.at[c, me_r, pl.ds(0, USED), :], rcv2.at[c, pl.ds(pl.multiple_of(me_r * SLOT, 8), USED), :], s2r.at[c]
        ).start()

    some_toeplitz(0, CUT_2)

    @pl.loop(0, nchunk)
    def _(c):
        arrived = rcv2.at[c, pl.ds(0, nrow * USED), :]
        pltpu.make_async_copy(arrived, arrived, s2r.at[c]).wait()
        states = [
            tuple(rcv2[c, pl.ds(s * V + m, KC, stride=SLOT), :] for s in range(4)) for m in range(V)
        ]
        f2 = [rcoef[2, m, pl.ds(c * KC, KC), :] for m in range(V)]

        def emit(r, z):
            z = [f2[m] * z[m] for m in range(V)]
            for m in range(V):
                total = None
                for n in range(V):
                    term = mcoef[r, pl.ds(pl.multiple_of((m * V + n) * K + c * KC, KC), KC), :] * z[n]
                    total = term if total is None else total + term
                xbuf[m, pl.ds(pl.multiple_of(r * KC, KC), KC), :] = total

        radial_pass(c, states, emit)

        def leaving(j, carry):
            total = jnp.zeros((RL, TL), F32)
            for kk in range(tile):
                k = c * KC + j * tile + kk
                field = [xbuf[m, pl.ds(j * tile + kk, RL, stride=KC), :] for m in range(V)]
                hi, lo = split(jnp.concatenate(field, axis=0))
                xsplit[k, :, 0:TL] = hi
                xsplit[k, :, TL : 2 * TL] = lo
                out = jnp.dot(
                    jnp.concatenate([hi, lo], axis=1), wturn[c * (KC // tile) + j], preferred_element_type=F32
                )
                out = out[:, 0:TL] + out[:, TL : 2 * TL]
                for m in range(V):
                    mine = (lane32 // LINE == kk) & (lane32 % 8 == m)
                    total = total + jnp.where(mine, out[m * RL : m * RL + RL], 0.0)
            tx1[pl.ds(c * (KC // tile) + j, RL, stride=8), :] = total
            return carry

        lax.fori_loop(0, KC // tile, leaving, 0, unroll=True)

    @pl.loop(0, nth - 1)
    def _(i):
        p = theta_peer(me_t, i, nth)
        pltpu.make_async_remote_copy(
            src_ref=tx1.at[pl.ds(pl.multiple_of(p * 8, 8), 8), :],
            dst_ref=trc1.at[me_t],
            send_sem=t1s,
            recv_sem=t1r,
            device_id={"theta": p},
            device_id_type=MESH,
        ).start()

    pltpu.make_async_copy(tx1.at[pl.ds(pl.multiple_of(me_t * 8, 8), 8), :], trc1.at[me_t], t1r).start()

    def local_solve(c):
        def solve(kk, carry):
            k = c * KC + kk
            for m in range(V):
                hi = xsplit[k, m * RL : m * RL + RL, 0:TL]
                lo = xsplit[k, m * RL : m * RL + RL, TL : 2 * TL]
                z = jnp.dot(jnp.concatenate([hi, lo], axis=0), gtab[k, m], preferred_element_type=F32)
                z = z[0:RL, 0:TL] + z[RL : 2 * RL, 0:TL] + z[0:RL, TL : 2 * TL]
                zbuf[m, pl.ds(pl.multiple_of(kk * RL, RL), RL), :] = z
            return carry

        lax.fori_loop(0, KC, solve, 0, unroll=4)

        def out_mix(kk, carry):
            rows = pl.ds(pl.multiple_of(kk * RL, RL), RL)
            field = mix(c * KC + kk, jnp.concatenate([zbuf[n, rows, :] for n in range(V)], axis=0))
            for m in range(V):
                l2[m, pl.ds(pl.multiple_of((c * KC + kk) * RL, RL), RL), :] = field[m * RL : m * RL + RL]
            return carry

        lax.fori_loop(0, KC, out_mix, 0, unroll=4)

    mrows[...] = jnp.zeros_like(mrows)
    for m in range(V):
        for n in range(V):
            mrows[pl.ds(m * K * 8 + n, K, stride=8), 0:RL] = mixo[m * V + n]
    group = 8 * TL // LINE
    source = lax.broadcasted_iota(jnp.int32, (TL, TL), 0)
    target = lax.broadcasted_iota(jnp.int32, (TL, TL), 1)
    source_rows = 8 * (target // LINE) + target % 8
    turned = []
    for m in range(V):
        for j in range(K * 8 // TL):
            turned.append(mrows[pl.ds(m * K * 8 + j * TL, TL), :].T[0:RL])
    hi, lo = split(jnp.concatenate(turned, axis=0))
    halves = jnp.concatenate([hi, lo], axis=1)
    for q in range(TL // group):
        pick = jnp.where(source == source_rows + q * group, 1.0, 0.0).astype(BF16)
        spread_rows = jnp.dot(halves, jnp.concatenate([pick, pick], axis=0), preferred_element_type=F32)
        for m in range(V):
            for j in range(K * 8 // TL):
                i = m * (K * 8 // TL) + j
                gain[j * (TL // group) + q, m * RL : m * RL + RL, :] = spread_rows[i * RL : i * RL + RL]

    for m in range(V):
        four = jnp.concatenate([mixo[m * V + n] for n in range(V - 1)], axis=1)
        last = mixo[m * V + V - 1]
        four_hi = four.astype(BF16).astype(F32)
        last_hi = last.astype(BF16).astype(F32)
        last = jnp.concatenate([last_hi, last_hi, last - last_hi, jnp.zeros_like(last)], axis=1)
        mflat[m] = jnp.concatenate([four_hi, four - four_hi, last], axis=1)

    @pl.loop(0, K)
    def _(k):
        for m in range(V):
            mcat[k, m] = jnp.broadcast_to(mflat[m, pl.ds(k, 1), :], (16, 3 * TL)).astype(BF16)

    some_toeplitz(CUT_2, K)

    u1, u2 = jnp.ones((8, TL), F32), jnp.ones((8, TL), F32)
    for kk in range(tile):
        for m in range(V):
            mine = (lane8 // LINE == kk) & (lane8 % 8 == m)
            u1 = jnp.where(mine, ucol[0, m, pl.ds(kk, 8, stride=tile), :], u1)
            u2 = jnp.where(mine, ucol[1, m, pl.ds(kk, 8, stride=tile), :], u2)
    a, b, cc = block_transfer(u1, u2, bits)[:3]
    around_1 = 1.0 / (1.0 - jnp.exp(-cells_t * u1))
    around_2 = 1.0 / (1.0 - jnp.exp(-cells_t * u2))
    pltpu.make_async_copy(trc1, trc1, t1r).wait()
    forward = lane8 % LINE < LINE // 2
    entering = [jnp.where(forward, trc1[i], trc1[nth - 1 - i]) for i in range(nth)]

    def cycle(rate, decay, around, terms):
        chain = [jnp.zeros((8, TL), F32)]
        for i in range(nth):
            chain.append(rate * chain[i] + terms[i])
        start = chain[nth] * around
        return [chain[i] + jnp.exp(-(TL * i) * decay) * start for i in range(nth)]

    one = cycle(a, u1, around_1, entering)
    two = cycle(b, u2, around_2, [entering[i] + cc * pltpu.roll(one[i], 8, 1) for i in range(nth)])
    even = lane8 // 8 % 2 == 0
    state = [jnp.where(even, one[i], two[i]) for i in range(nth)]
    for d in range(nth):
        tx2[d] = jnp.where(forward, state[d], state[nth - 1 - d])

    @pl.loop(0, nth - 1)
    def _(i):
        d = theta_peer(me_t, i, nth)
        pltpu.make_async_remote_copy(
            src_ref=tx2.at[d],
            dst_ref=infl.at[pl.ds(pl.multiple_of(me_t * 8, 8), 8), :],
            send_sem=t2s,
            recv_sem=t2r,
            device_id={"theta": d},
            device_id_type=MESH,
        ).start()

    pltpu.make_async_copy(tx2.at[me_t], infl.at[pl.ds(pl.multiple_of(me_t * 8, 8), 8), :], t2r).start()

    @pl.loop(0, nchunk)
    def _(c):
        local_solve(c)

    pltpu.make_async_copy(infl, infl, t2r).wait()

    @pl.loop(0, nchunk)
    def _(c):
        sent = rcv1.at[c, pl.ds(0, nrow - 1), pl.ds(0, USED), :]
        pltpu.make_async_copy(sent, sent, s1s.at[c]).wait()
        pltpu.make_async_copy(sent, sent, s2s.at[c]).wait()

    sent = trc1.at[pl.ds(0, nth - 1)]
    pltpu.make_async_copy(sent, sent, t1s).wait()
    pltpu.make_async_copy(sent, sent, t2s).wait()


def finish_kernel(sizes, l2, infl, etab, gain, out, buf, sem):
    V, K, RL, TL, nrow, nth = sizes
    tile = TL // LINE
    kr = tile * RL
    row = lax.broadcasted_iota(jnp.int32, (TL, TL), 0) // LINE

    def out_copy(j):
        rows = pl.ds(pl.multiple_of(j * kr, kr), kr)
        return pltpu.make_async_copy(buf.at[:, rows, :], out.at[:, rows, :], sem.at[j])

    @pl.loop(0, K // tile)
    def _(j):
        state = infl[pl.ds(j, RL, stride=8), :]
        hi, lo = split(gain[j] * jnp.concatenate([state] * V, axis=0))
        left = jnp.concatenate([hi, lo], axis=1)
        response = etab[pl.ds(pl.multiple_of(j * TL, TL), TL), :]
        for kk in range(tile):
            ehi, elo = split(jnp.where(row == kk, response, 0.0))
            right = jnp.concatenate(
                [jnp.concatenate([ehi, ehi], axis=0), jnp.concatenate([elo, jnp.zeros_like(elo)], axis=0)], axis=1
            )
            inflow = jnp.dot(left, right, preferred_element_type=F32)
            inflow = inflow[:, 0:TL] + inflow[:, TL : 2 * TL]
            rows = pl.ds(pl.multiple_of(j * kr + kk * RL, RL), RL)
            for m in range(V):
                buf[m, rows, :] = l2[m, rows, :] + inflow[m * RL : m * RL + RL]
        out_copy(j).start()

    @pl.loop(0, K // tile)
    def _(j):
        out_copy(j).wait()


def body(nrow, nth, rhs, dr, dt, mixm, mixo):
    V, K, RL, TL = rhs.shape
    sizes = (V, K, RL, TL, nrow, nth)
    nchunk = K // KC
    kr = KC * RL
    field = jax.ShapeDtypeStruct((V, K * RL, TL), F32)
    vmem = pl.BlockSpec(memory_space=pltpu.VMEM)
    hbm = pl.BlockSpec(memory_space=pl.ANY)
    mixm = mixm.reshape(V * V, K, RL)
    mixo = mixo.reshape(V * V, K, RL)
    dma = pltpu.SemaphoreType.DMA
    nline = K * LINE // TL
    l2, infl, etab, gain = pl.pallas_call(
        functools.partial(solve_kernel, sizes),
        out_shape=(
            pltpu.VMEM((V, K * RL, TL), F32),
            pltpu.VMEM((nth * 8, TL), F32),
            pltpu.VMEM((K * LINE, TL), F32),
            pltpu.VMEM((nline, V * RL, TL), F32),
        ),
        in_specs=[pl.BlockSpec(memory_space=pltpu.HBM), vmem, vmem, vmem, vmem],
        out_specs=(vmem, vmem, vmem, vmem),
        scratch_shapes=[
            pltpu.VMEM((nchunk, V, kr, TL), F32),
            pltpu.VMEM((V, kr, TL), F32),
            pltpu.VMEM((V, kr, TL), F32),
            pltpu.VMEM((V, kr, TL), F32),
            pltpu.VMEM((3, V, K, TL), F32),
            pltpu.VMEM((2, V, K, TL), F32),
            pltpu.VMEM((V, K, TL), F32),
            pltpu.VMEM((V, K, TL), F32),
            pltpu.VMEM((K * LINE, TL), F32),
            pltpu.VMEM((nline, 2 * TL, 2 * TL), BF16),
            pltpu.VMEM((K, V, TL, 2 * TL), BF16),
            pltpu.VMEM((RL, V * V * K, TL), F32),
            pltpu.VMEM((V, K, 3 * TL), F32),
            pltpu.VMEM((K, V, 16, 3 * TL), BF16),
            pltpu.VMEM((V * K * 8, TL), F32),
            pltpu.VMEM((K, V * RL, 2 * TL), BF16),
            pltpu.VMEM((nchunk, V, kr, TL), F32),
            pltpu.VMEM((nchunk, nrow * SLOT, TL), F32),
            pltpu.VMEM((nchunk, nrow, SLOT, TL), F32),
            pltpu.VMEM((nchunk, nrow, SLOT, TL), F32),
            pltpu.VMEM((nchunk, nrow * SLOT, TL), F32),
            pltpu.VMEM((RL * 8, TL), F32),
            pltpu.VMEM((nth, 8, TL), F32),
            pltpu.VMEM((nth, 8, TL), F32),
            dma((nchunk,)), dma((nchunk,)), dma((nchunk,)), dma((nchunk,)), dma((nchunk,)),
            dma, dma, dma, dma,
        ],
        compiler_params=pltpu.CompilerParams(
            collective_id=0, has_side_effects=True, vmem_limit_bytes=58 * 1024 * 1024
        ),
        name="solve",
    )(rhs.reshape(V, K * RL, TL), jnp.swapaxes(dr, 0, 1), jnp.swapaxes(dt, 0, 1), mixm, mixo)
    out = pl.pallas_call(
        functools.partial(finish_kernel, sizes),
        out_shape=field,
        in_specs=[vmem, vmem, vmem, vmem],
        out_specs=hbm,
        scratch_shapes=[pltpu.VMEM((V, K * RL, TL), F32), dma((K * LINE // TL,))],
        compiler_params=pltpu.CompilerParams(vmem_limit_bytes=16 * 1024 * 1024),
        name="finish",
    )(l2, infl, etab, gain)
    return out.reshape(V, K, RL, TL)


def solution(mesh):
    return jax.shard_map(
        functools.partial(body, mesh.shape["row"], mesh.shape["theta"]),
        mesh=mesh,
        in_specs=(
            P(None, None, "row", "theta"),
            P(),
            P(),
            P(None, None, None, "row"),
            P(None, None, None, "row"),
        ),
        out_specs=P(None, None, "row", "theta"),
        check_vma=False,
    )
```

```python
import functools

import jax
import jax.numpy as jnp
from jax import lax
from jax.experimental import pallas as pl
from jax.experimental.pallas import tpu as pltpu
from jax.sharding import PartitionSpec as P

MESH = pl.DeviceIdType.MESH
KC = 8
SLOT, USED = 24, 20
STATES = 4
CUT_2 = 12
LINE = 32
F32 = jnp.float32
BF16 = jnp.bfloat16


def row_peer(me, i, n):
    half = n // 2
    step = jnp.where(i < half, i, i - half)
    shift = lax.rem(half // 2 + jnp.where(step % 2 == 0, half - step // 2, (step + 1) // 2), half)
    side = jnp.where(i < half, me // half + 1, me // half) % 2
    return side * half + lax.rem(me + shift, half)


def theta_peer(me, i, n):
    return lax.rem(me + n // 2 + jnp.where(i % 2 == 0, n - i // 2, (i + 1) // 2), n)


def gap(u):
    h = 0.5 * u
    q = h * h
    series = 1.0 + q / 6.0 * (1.0 + q / 20.0 * (1.0 + q / 42.0 * (1.0 + q / 72.0)))
    return 2.0 * jnp.exp(-h) * h * series


def split(x):
    hi = x.astype(BF16)
    return hi, (x - hi.astype(F32)).astype(BF16)


def block_transfer(u1, u2, doublings):
    a, b = jnp.exp(-u1), jnp.exp(-u2)
    c = a
    q11, q12, q21, q22 = a, b, a, b
    for _ in range(doublings):
        x11, x12 = q11 * a + q12 * c, q12 * b
        x21, x22 = q21 * a + q22 * c, q22 * b
        q11, q12, q21, q22 = (
            q11 + a * x11,
            q12 + a * x12,
            q21 + c * x11 + b * x21,
            q22 + c * x12 + b * x22,
        )
        c = c * (a + b)
        a, b = a * a, b * b
    return a, b, c, q11, q12, q21, q22


def pick_lane(values, index):
    lane = lax.broadcasted_iota(jnp.int32, values.shape, 1)
    return jnp.sum(jnp.where(lane == index, values, 0.0), axis=1, keepdims=True)


def power_tables(u1, u2, n, bits):
    nf = n.astype(F32)
    a, b = jnp.exp(-nf * u1), jnp.exp(-nf * u2)
    ab, bb = jnp.exp(-u1), jnp.exp(-u2)
    pb = jnp.ones_like(ab)
    p = jnp.zeros_like(nf * u1)
    low = jnp.ones_like(p)
    for bit in range(bits):
        has = (n >> bit) & 1 == 1
        p = jnp.where(has, ab * p + low * pb, p)
        low = jnp.where(has, low * bb, low)
        pb = pb * (ab + bb)
        ab, bb = ab * ab, bb * bb
    return a, b, p


def solve_kernel(
    sizes, rhs, decay_r, decay_t, mixm, mixo, l2, infl, etab, gain,
    xin, xbuf, zbuf, ybuf, rcoef, ucol, h0tab, h1tab, wtab, wturn, gtab, mcoef, mflat, mcat, mrows, xsplit, xt,
    e1, rcv1, o1, rcv2, tx1, trc1, tx2,
    in_sem, s1s, s1r, s2s, s2r, t1s, t1r, t2s, t2r,
):
    V, K, RL, TL, nrow, nth = sizes
    nchunk = K // KC
    me_r = lax.axis_index("row")
    me_t = lax.axis_index("theta")
    kr = KC * RL
    dr = [decay_r[:, j, :] for j in range(2)]
    dt = [decay_t[:, j, :] for j in range(2)]

    def in_copy(c):
        return pltpu.make_async_copy(rhs.at[:, pl.ds(c * kr, kr), :], xin.at[c], in_sem.at[c])

    for c in range(nchunk):
        in_copy(c).start()

    barrier = pltpu.get_barrier_semaphore()

    @pl.loop(0, nth - 1)
    def _(i):
        pl.semaphore_signal(barrier, inc=1, device_id={"theta": theta_peer(me_t, i, nth)}, device_id_type=MESH)

    @pl.loop(0, nrow - 1)
    def _(i):
        pl.semaphore_signal(barrier, inc=1, device_id={"row": row_peer(me_r, i, nrow)}, device_id_type=MESH)

    cells_r = RL * nrow
    ur1, ur2 = dr[0] / cells_r, dr[1] / cells_r
    fr = gap(ur1) * gap(ur2)
    diag = lax.broadcasted_iota(jnp.int32, (K, K), 0) == lax.broadcasted_iota(jnp.int32, (K, K), 1)

    def to_columns(table, ref, j):
        for m in range(V):
            column = jnp.sum(
                jnp.where(diag, jnp.broadcast_to(table[m : m + 1, :], (K, K)), 0.0), axis=1, keepdims=True
            )
            ref[j, m] = jnp.broadcast_to(column, (K, TL))

    for j, table in enumerate((jnp.exp(-ur1), jnp.exp(-ur2), fr * fr)):
        to_columns(table, rcoef, j)
    radial_block = block_transfer(ur1, ur2, RL.bit_length() - 1)

    def radial_pass(c, states, emit):
        r1 = [rcoef[0, m, pl.ds(c * KC, KC), :] for m in range(V)]
        r2 = [rcoef[1, m, pl.ds(c * KC, KC), :] for m in range(V)]

        def ahead(r, carry):
            out = []
            for m in range(V):
                s1, s2 = carry[m]
                s1 = r1[m] * s1 + xt[c, m, pl.ds(pl.multiple_of(r * KC, KC), KC), :]
                s2 = r2[m] * s2 + s1
                ybuf[m, pl.ds(pl.multiple_of(r * KC, KC), KC), :] = s2
                out.append((s1, s2))
            return tuple(out)

        def behind(i, carry):
            r = RL - 1 - i
            out = []
            for m in range(V):
                u1, u2 = carry[m]
                u1 = r1[m] * u1 + ybuf[m, pl.ds(pl.multiple_of(r * KC, KC), KC), :]
                u2 = r2[m] * u2 + u1
                out.append((u1, u2))
            if emit is not None:
                emit(r, [pair[1] for pair in out])
            return tuple(out)

        first = lax.fori_loop(0, RL, ahead, tuple((s[0], s[1]) for s in states), unroll=8)
        second = lax.fori_loop(0, RL, behind, tuple((s[2], s[3]) for s in states), unroll=8)
        return first, second

    @pl.loop(0, nchunk)
    def _(c):
        in_copy(c).wait()

        @pl.loop(0, V)
        def _(m):
            for kk in range(KC):
                for q in range(RL // 8):
                    first_row = kk * RL + q * 8
                    xt[c, m, pl.ds(q * 8 * KC + kk, 8, stride=KC), :] = xin[c, m, first_row : first_row + 8, :]

        zero = jnp.zeros((KC, TL), F32)
        first, second = radial_pass(c, [(zero,) * 4] * V, None)
        for m in range(V):
            for s, value in enumerate((first[m][0], first[m][1], second[m][0], second[m][1])):
                e1[c, pl.ds(s * V + m, KC, stride=SLOT), :] = value

    pl.semaphore_wait(barrier, nrow - 1 + nth - 1)

    @pl.loop(0, nchunk)
    def _(c):
        @pl.loop(0, nrow - 1)
        def _(i):
            p = row_peer(me_r, i, nrow)
            pltpu.make_async_remote_copy(
                src_ref=e1.at[c, pl.ds(pl.multiple_of(p * SLOT, 8), USED), :],
                dst_ref=rcv1.at[c, me_r, pl.ds(0, USED), :],
                send_sem=s1s.at[c],
                recv_sem=s1r.at[c],
                device_id={"row": p},
                device_id_type=MESH,
            ).start()

        pltpu.make_async_copy(
            e1.at[c, pl.ds(pl.multiple_of(me_r * SLOT, 8), USED), :], rcv1.at[c, me_r, pl.ds(0, USED), :], s1r.at[c]
        ).start()

    cells_t = TL * nth
    ut1, ut2 = dt[0] / cells_t, dt[1] / cells_t
    to_columns(ut1, ucol, 0)
    to_columns(ut2, ucol, 1)
    lane32 = lax.broadcasted_iota(jnp.int32, (RL, TL), 1)
    lane8 = lax.broadcasted_iota(jnp.int32, (8, TL), 1)
    bits = TL.bit_length() - 1
    etab[...] = jnp.zeros_like(etab)
    wtab[...] = jnp.zeros_like(wtab)

    def tables(q, carry):
        m, c = q // nchunk, q % nchunk
        rows = pl.ds(pl.multiple_of(c * KC, KC), KC)
        u1, u2 = ucol[0, m, rows, :], ucol[1, m, rows, :]
        r1, r2 = jnp.exp(-u1), jnp.exp(-u2)
        f = gap(u1) * gap(u2)
        i12, i11, i22 = 1.0 / gap(u1 + u2), 1.0 / gap(2.0 * u1), 1.0 / gap(2.0 * u2)
        scale_1 = f * f * r1 * i12
        coef_a = scale_1 * i12 * (r1 * i11 + r2 * i22)
        coef_p = scale_1 * i22
        coef_b = f * f * i12 * i22
        af, bf, pf = power_tables(u1, u2, lane8, bits)
        ar, br, pr = power_tables(u1, u2, TL - 1 - lane8, bits)
        pf1, pr1 = r1 * pf + bf, r1 * pr + br
        e_t1 = coef_a * (r1 * ar) + coef_p * pr1
        e_t2 = coef_b * (r2 * br)
        h0tab[m, rows, :] = coef_a * af + coef_p * pf + coef_b * bf
        h1tab[m, rows, :] = e_t1 + e_t2
        e_s1 = coef_a * (r1 * af) + coef_p * pf1
        e_s2 = coef_b * (r2 * bf)
        for s, value in enumerate((e_s1, e_s2, e_t1, e_t2)):
            etab[pl.ds(c * KC * 32 + 8 * s + m, KC, stride=32), :] = value
        for s, value in enumerate((ar, pr1, af, pf1)):
            wtab[pl.ds(c * KC * 32 + 8 * s + m, KC, stride=32), :] = value
        return carry

    lax.fori_loop(0, V * nchunk, tables, 0, unroll=2)

    tile = TL // LINE

    scaled = [mixm[m * V + n] * rcoef[2, n][:, 0:RL] for m in range(V) for n in range(V)]
    hi, lo = split(jnp.concatenate(scaled, axis=0))
    halves = jnp.concatenate([hi, lo], axis=1)
    pick_row = lax.broadcasted_iota(jnp.int32, (2 * RL, 2 * TL), 0) % RL
    pick_half = lax.broadcasted_iota(jnp.int32, (2 * RL, 2 * TL), 1) // TL

    @pl.loop(0, RL // 2)
    def _(i):
        pick = jnp.where(pick_row == 2 * i + pick_half, 1.0, 0.0).astype(BF16)
        both = jnp.dot(halves, pick, preferred_element_type=F32)
        mcoef[2 * i] = both[:, 0:TL]
        mcoef[2 * i + 1] = both[:, TL : 2 * TL]

    row16 = lax.broadcasted_iota(jnp.int32, (16, 3 * TL), 0)
    col16 = lax.broadcasted_iota(jnp.int32, (16, 3 * TL), 1) % RL
    on_diagonal = [jnp.where(row16 + 16 * half == col16, 1.0, 0.0).astype(BF16) for half in range(RL // 16)]

    def mix(k, field):
        hi, lo = split(field)
        four = (V - 1) * RL
        right = jnp.concatenate(
            [hi[0:four], lo[0:four], hi[0:four], hi[four:], lo[four:], hi[four:], jnp.zeros((RL, TL), BF16)], axis=0
        )
        left = jnp.concatenate([mcat[k, m] * mask for m in range(V) for mask in on_diagonal], axis=0)
        left = jnp.concatenate([left[:, 0:TL], left], axis=1)
        return jnp.dot(left, right, preferred_element_type=F32)

    lane16 = lax.broadcasted_iota(jnp.int32, (16, TL), 1)
    sub16 = lax.broadcasted_iota(jnp.int32, (16, TL), 0)

    def toeplitz(k):
        for m in range(V):
            near = pltpu.roll(jnp.broadcast_to(h0tab[m, pl.ds(k, 1), :], (16, TL)), 0, 1, stride=1, stride_axis=0)
            far = pltpu.roll(jnp.broadcast_to(h1tab[m, pl.ds(k, 1), :], (16, TL)), 0, 1, stride=1, stride_axis=0)
            near = jnp.where(lane16 < sub16, far, near)
            for part, (n, f) in enumerate(zip(split(near), split(far))):
                for b in range(TL // 16):
                    rows = pltpu.roll(jnp.where(lane16 >= TL - 16 * b, f, n), 16 * b, 1) if b else n
                    gtab[k, m, 16 * b : 16 * b + 16, part * TL : part * TL + TL] = rows

    def some_toeplitz(first, last):
        @pl.loop(first, last)
        def _(k):
            toeplitz(k)

    @pl.loop(0, nchunk)
    def _(c):
        a, b, cc, q11, q12, q21, q22 = (
            jnp.broadcast_to(pick_lane(x, c * KC + me_r), (V, TL)) for x in radial_block
        )
        arrived = rcv1.at[c, :, pl.ds(0, USED), :]
        pltpu.make_async_copy(arrived, arrived, s1r.at[c]).wait()

        def got(d, s):
            return rcv1[c, d, s * V : s * V + V, :]

        zero = jnp.zeros((V, TL), F32)
        sa, sb = [zero], [zero]
        for d in range(nrow - 1):
            sa.append(a * sa[d] + got(d, 0))
            sb.append(b * sb[d] + cc * sa[d] + got(d, 1))
        ta, tb = zero, zero
        for d in range(nrow - 1, -1, -1):
            for s, value in enumerate((sa[d], sb[d], ta, tb)):
                o1[c, d, s * V : s * V + V, :] = value
            if d:
                ta, tb = (
                    a * ta + got(d, 2) + q11 * sa[d] + q12 * sb[d],
                    b * tb + cc * ta + got(d, 3) + q21 * sa[d] + q22 * sb[d],
                )

        @pl.loop(0, nrow - 1)
        def _(i):
            p = row_peer(me_r, i, nrow)
            pltpu.make_async_remote_copy(
                src_ref=o1.at[c, p, pl.ds(0, USED), :],
                dst_ref=rcv2.at[c, pl.ds(pl.multiple_of(me_r * SLOT, 8), USED), :],
                send_sem=s2s.at[c],
                recv_sem=s2r.at[c],
                device_id={"row": p},
                device_id_type=MESH,
            ).start()

        pltpu.make_async_copy(
            o1.at[c, me_r, pl.ds(0, USED), :], rcv2.at[c, pl.ds(pl.multiple_of(me_r * SLOT, 8), USED), :], s2r.at[c]
        ).start()

    some_toeplitz(0, CUT_2)

    for j in range(K // tile):
        hi, lo = split(wtab[j * TL : (j + 1) * TL, :].T)
        wturn[j] = jnp.concatenate(
            [jnp.concatenate([hi, hi], axis=0), jnp.concatenate([lo, jnp.zeros_like(lo)], axis=0)], axis=1
        )

    @pl.loop(0, nchunk)
    def _(c):
        arrived = rcv2.at[c, pl.ds(0, nrow * USED), :]
        pltpu.make_async_copy(arrived, arrived, s2r.at[c]).wait()
        states = [
            tuple(rcv2[c, pl.ds(s * V + m, KC, stride=SLOT), :] for s in range(4)) for m in range(V)
        ]

        def emit(r, z):
            for m in range(V):
                total = None
                for n in range(V):
                    term = mcoef[r, pl.ds(pl.multiple_of((m * V + n) * K + c * KC, KC), KC), :] * z[n]
                    total = term if total is None else total + term
                xbuf[m, pl.ds(pl.multiple_of(r * KC, KC), KC), :] = total

        radial_pass(c, states, emit)

        def leaving(j, carry):
            total = jnp.zeros((RL, TL), F32)
            for kk in range(tile):
                k = c * KC + j * tile + kk
                field = [xbuf[m, pl.ds(j * tile + kk, RL, stride=KC), :] for m in range(V)]
                hi, lo = split(jnp.concatenate(field, axis=0))
                xsplit[k, :, 0:TL] = hi
                xsplit[k, :, TL : 2 * TL] = lo
                out = jnp.dot(
                    jnp.concatenate([hi, lo], axis=1), wturn[c * (KC // tile) + j], preferred_element_type=F32
                )
                out = out[:, 0:TL] + out[:, TL : 2 * TL]
                for m in range(V):
                    mine = (lane32 // LINE == kk) & (lane32 % 8 == m)
                    total = total + jnp.where(mine, out[m * RL : m * RL + RL], 0.0)
            tx1[pl.ds(c * (KC // tile) + j, RL, stride=8), :] = total
            return carry

        lax.fori_loop(0, KC // tile, leaving, 0, unroll=True)

    @pl.loop(0, nth - 1)
    def _(i):
        p = theta_peer(me_t, i, nth)
        pltpu.make_async_remote_copy(
            src_ref=tx1.at[pl.ds(pl.multiple_of(p * 8, 8), 8), :],
            dst_ref=trc1.at[me_t],
            send_sem=t1s,
            recv_sem=t1r,
            device_id={"theta": p},
            device_id_type=MESH,
        ).start()

    pltpu.make_async_copy(tx1.at[pl.ds(pl.multiple_of(me_t * 8, 8), 8), :], trc1.at[me_t], t1r).start()

    def local_solve(c):
        def solve(kk, carry):
            k = c * KC + kk
            for m in range(V):
                hi = xsplit[k, m * RL : m * RL + RL, 0:TL]
                lo = xsplit[k, m * RL : m * RL + RL, TL : 2 * TL]
                z = jnp.dot(jnp.concatenate([hi, lo], axis=0), gtab[k, m], preferred_element_type=F32)
                z = z[0:RL, 0:TL] + z[RL : 2 * RL, 0:TL] + z[0:RL, TL : 2 * TL]
                zbuf[m, pl.ds(pl.multiple_of(kk * RL, RL), RL), :] = z
            return carry

        lax.fori_loop(0, KC, solve, 0, unroll=4)

        def out_mix(kk, carry):
            rows = pl.ds(pl.multiple_of(kk * RL, RL), RL)
            field = mix(c * KC + kk, jnp.concatenate([zbuf[n, rows, :] for n in range(V)], axis=0))
            for m in range(V):
                l2[m, pl.ds(pl.multiple_of((c * KC + kk) * RL, RL), RL), :] = field[m * RL : m * RL + RL]
            return carry

        lax.fori_loop(0, KC, out_mix, 0, unroll=4)

    mrows[...] = jnp.zeros_like(mrows)
    for m in range(V):
        for n in range(V):
            mrows[pl.ds(m * K * 8 + n, K, stride=8), 0:RL] = mixo[m * V + n]
    group = 8 * TL // LINE
    source = lax.broadcasted_iota(jnp.int32, (TL, TL), 0)
    target = lax.broadcasted_iota(jnp.int32, (TL, TL), 1)
    source_rows = 8 * (target // LINE) + target % 8
    turned = []
    for m in range(V):
        for j in range(K * 8 // TL):
            turned.append(mrows[pl.ds(m * K * 8 + j * TL, TL), :].T[0:RL])
    hi, lo = split(jnp.concatenate(turned, axis=0))
    halves = jnp.concatenate([hi, lo], axis=1)
    for q in range(TL // group):
        pick = jnp.where(source == source_rows + q * group, 1.0, 0.0).astype(BF16)
        spread_rows = jnp.dot(halves, jnp.concatenate([pick, pick], axis=0), preferred_element_type=F32)
        for m in range(V):
            for j in range(K * 8 // TL):
                i = m * (K * 8 // TL) + j
                gain[j * (TL // group) + q, m * RL : m * RL + RL, :] = spread_rows[i * RL : i * RL + RL]

    for m in range(V):
        four = jnp.concatenate([mixo[m * V + n] for n in range(V - 1)], axis=1)
        last = mixo[m * V + V - 1]
        four_hi = four.astype(BF16).astype(F32)
        last_hi = last.astype(BF16).astype(F32)
        last = jnp.concatenate([last_hi, last_hi, last - last_hi, jnp.zeros_like(last)], axis=1)
        mflat[m] = jnp.concatenate([four_hi, four - four_hi, last], axis=1)

    @pl.loop(0, K)
    def _(k):
        for m in range(V):
            mcat[k, m] = jnp.broadcast_to(mflat[m, pl.ds(k, 1), :], (16, 3 * TL)).astype(BF16)

    some_toeplitz(CUT_2, K)

    u1, u2 = jnp.ones((8, TL), F32), jnp.ones((8, TL), F32)
    for kk in range(tile):
        for m in range(V):
            mine = (lane8 // LINE == kk) & (lane8 % 8 == m)
            u1 = jnp.where(mine, ucol[0, m, pl.ds(kk, 8, stride=tile), :], u1)
            u2 = jnp.where(mine, ucol[1, m, pl.ds(kk, 8, stride=tile), :], u2)
    a, b, cc = block_transfer(u1, u2, bits)[:3]
    around_1 = 1.0 / (1.0 - jnp.exp(-cells_t * u1))
    around_2 = 1.0 / (1.0 - jnp.exp(-cells_t * u2))
    pltpu.make_async_copy(trc1, trc1, t1r).wait()
    forward = lane8 % LINE < LINE // 2
    entering = [jnp.where(forward, trc1[i], trc1[nth - 1 - i]) for i in range(nth)]

    def cycle(rate, decay, around, terms):
        chain = [jnp.zeros((8, TL), F32)]
        for i in range(nth):
            chain.append(rate * chain[i] + terms[i])
        start = chain[nth] * around
        return [chain[i] + jnp.exp(-(TL * i) * decay) * start for i in range(nth)]

    one = cycle(a, u1, around_1, entering)
    two = cycle(b, u2, around_2, [entering[i] + cc * pltpu.roll(one[i], 8, 1) for i in range(nth)])
    even = lane8 // 8 % 2 == 0
    state = [jnp.where(even, one[i], two[i]) for i in range(nth)]
    for d in range(nth):
        tx2[d] = jnp.where(forward, state[d], state[nth - 1 - d])

    @pl.loop(0, nth - 1)
    def _(i):
        d = theta_peer(me_t, i, nth)
        pltpu.make_async_remote_copy(
            src_ref=tx2.at[d],
            dst_ref=infl.at[pl.ds(pl.multiple_of(me_t * 8, 8), 8), :],
            send_sem=t2s,
            recv_sem=t2r,
            device_id={"theta": d},
            device_id_type=MESH,
        ).start()

    pltpu.make_async_copy(tx2.at[me_t], infl.at[pl.ds(pl.multiple_of(me_t * 8, 8), 8), :], t2r).start()

    @pl.loop(0, nchunk)
    def _(c):
        local_solve(c)

    pltpu.make_async_copy(infl, infl, t2r).wait()

    @pl.loop(0, nchunk)
    def _(c):
        sent = rcv1.at[c, pl.ds(0, nrow - 1), pl.ds(0, USED), :]
        pltpu.make_async_copy(sent, sent, s1s.at[c]).wait()
        pltpu.make_async_copy(sent, sent, s2s.at[c]).wait()

    sent = trc1.at[pl.ds(0, nth - 1)]
    pltpu.make_async_copy(sent, sent, t1s).wait()
    pltpu.make_async_copy(sent, sent, t2s).wait()


def finish_kernel(sizes, l2, infl, etab, gain, out, buf, sem):
    V, K, RL, TL, nrow, nth = sizes
    tile = TL // LINE
    kr = tile * RL
    row = lax.broadcasted_iota(jnp.int32, (TL, TL), 0) // LINE

    def out_copy(j):
        rows = pl.ds(pl.multiple_of(j * kr, kr), kr)
        return pltpu.make_async_copy(buf.at[:, rows, :], out.at[:, rows, :], sem.at[j])

    @pl.loop(0, K // tile)
    def _(j):
        state = infl[pl.ds(j, RL, stride=8), :]
        hi, lo = split(gain[j] * jnp.concatenate([state] * V, axis=0))
        left = jnp.concatenate([hi, lo], axis=1)
        response = etab[pl.ds(pl.multiple_of(j * TL, TL), TL), :]
        for kk in range(tile):
            ehi, elo = split(jnp.where(row == kk, response, 0.0))
            right = jnp.concatenate(
                [jnp.concatenate([ehi, ehi], axis=0), jnp.concatenate([elo, jnp.zeros_like(elo)], axis=0)], axis=1
            )
            inflow = jnp.dot(left, right, preferred_element_type=F32)
            inflow = inflow[:, 0:TL] + inflow[:, TL : 2 * TL]
            rows = pl.ds(pl.multiple_of(j * kr + kk * RL, RL), RL)
            for m in range(V):
                buf[m, rows, :] = l2[m, rows, :] + inflow[m * RL : m * RL + RL]
        out_copy(j).start()

    @pl.loop(0, K // tile)
    def _(j):
        out_copy(j).wait()


def body(nrow, nth, rhs, dr, dt, mixm, mixo):
    V, K, RL, TL = rhs.shape
    sizes = (V, K, RL, TL, nrow, nth)
    nchunk = K // KC
    kr = KC * RL
    field = jax.ShapeDtypeStruct((V, K * RL, TL), F32)
    vmem = pl.BlockSpec(memory_space=pltpu.VMEM)
    hbm = pl.BlockSpec(memory_space=pl.ANY)
    mixm = mixm.reshape(V * V, K, RL)
    mixo = mixo.reshape(V * V, K, RL)
    dma = pltpu.SemaphoreType.DMA
    nline = K * LINE // TL
    l2, infl, etab, gain = pl.pallas_call(
        functools.partial(solve_kernel, sizes),
        out_shape=(
            pltpu.VMEM((V, K * RL, TL), F32),
            pltpu.VMEM((nth * 8, TL), F32),
            pltpu.VMEM((K * LINE, TL), F32),
            pltpu.VMEM((nline, V * RL, TL), F32),
        ),
        in_specs=[pl.BlockSpec(memory_space=pltpu.HBM), vmem, vmem, vmem, vmem],
        out_specs=(vmem, vmem, vmem, vmem),
        scratch_shapes=[
            pltpu.VMEM((nchunk, V, kr, TL), F32),
            pltpu.VMEM((V, kr, TL), F32),
            pltpu.VMEM((V, kr, TL), F32),
            pltpu.VMEM((V, kr, TL), F32),
            pltpu.VMEM((3, V, K, TL), F32),
            pltpu.VMEM((2, V, K, TL), F32),
            pltpu.VMEM((V, K, TL), F32),
            pltpu.VMEM((V, K, TL), F32),
            pltpu.VMEM((K * LINE, TL), F32),
            pltpu.VMEM((nline, 2 * TL, 2 * TL), BF16),
            pltpu.VMEM((K, V, TL, 2 * TL), BF16),
            pltpu.VMEM((RL, V * V * K, TL), F32),
            pltpu.VMEM((V, K, 3 * TL), F32),
            pltpu.VMEM((K, V, 16, 3 * TL), BF16),
            pltpu.VMEM((V * K * 8, TL), F32),
            pltpu.VMEM((K, V * RL, 2 * TL), BF16),
            pltpu.VMEM((nchunk, V, kr, TL), F32),
            pltpu.VMEM((nchunk, nrow * SLOT, TL), F32),
            pltpu.VMEM((nchunk, nrow, SLOT, TL), F32),
            pltpu.VMEM((nchunk, nrow, SLOT, TL), F32),
            pltpu.VMEM((nchunk, nrow * SLOT, TL), F32),
            pltpu.VMEM((RL * 8, TL), F32),
            pltpu.VMEM((nth, 8, TL), F32),
            pltpu.VMEM((nth, 8, TL), F32),
            dma((nchunk,)), dma((nchunk,)), dma((nchunk,)), dma((nchunk,)), dma((nchunk,)),
            dma, dma, dma, dma,
        ],
        compiler_params=pltpu.CompilerParams(
            collective_id=0, has_side_effects=True, vmem_limit_bytes=58 * 1024 * 1024
        ),
        name="solve",
    )(rhs.reshape(V, K * RL, TL), jnp.swapaxes(dr, 0, 1), jnp.swapaxes(dt, 0, 1), mixm, mixo)
    out = pl.pallas_call(
        functools.partial(finish_kernel, sizes),
        out_shape=field,
        in_specs=[vmem, vmem, vmem, vmem],
        out_specs=hbm,
        scratch_shapes=[pltpu.VMEM((V, K * RL, TL), F32), dma((K * LINE // TL,))],
        compiler_params=pltpu.CompilerParams(vmem_limit_bytes=16 * 1024 * 1024),
        name="finish",
    )(l2, infl, etab, gain)
    return out.reshape(V, K, RL, TL)


def solution(mesh):
    return jax.shard_map(
        functools.partial(body, mesh.shape["row"], mesh.shape["theta"]),
        mesh=mesh,
        in_specs=(
            P(None, None, "row", "theta"),
            P(),
            P(),
            P(None, None, None, "row"),
            P(None, None, None, "row"),
        ),
        out_specs=P(None, None, "row", "theta"),
        check_vma=False,
    )
```
